128 devices in a mesh: seq: 32 (over z, x, core), section: 4 (over y).
Axes of the slice: x: 4, y: 4, z: 4, core: 2. Of those that a mesh axis runs over, the one named last changes fastest.
Arguments:
- layer_in: bfloat16 [4, 8192, 3072], P('section', 'seq'), may hold values from -6 to 6
- norm_gain: float32 [4, 3072], P('section'), may hold values from 0.1 to 1.9
- conv_weight: float32 [4, 3, 3072], P('section'), may hold values from -3.5 to 3.5
- query_weight: bfloat16 [4, 3072, 384], P('section'), may hold values from -0.109375 to 0.109375
- key_weight: bfloat16 [4, 3072, 384], P('section'), may hold values from -0.109375 to 0.109375
- out_gain: float32 [4, 3072], P('section'), may hold values from 0.1 to 1.9
- layer_grad: bfloat16 [4, 8192, 3072], P('section', 'seq'), may hold values from -6 to 6
Outputs:
- next_input: bfloat16 [4, 8192, 3072], P('section', 'seq')
- prev_grad: bfloat16 [4, 8192, 3072], P('section', 'seq')
The draws below stay inside these ranges and needn't reach their ends.
All inputs are finite; a program needn't handle non-finite values.
Results may differ from the reference program's by a relative error of at most 0.03.
Values may be sent and summed in bfloat16 or wider, within the bound.
No kernel may reach another device: no remote copies, remote signals or barrier semaphores. Data moves between devices by JAX's collectives and lax.ppermute only.
A program may use at most 192 MiB of HBM per device.

```python
import math
import jax
import jax.numpy as jnp
from jax import lax

HEADS = 24
FEAT = 16
VDIM = 128
CONV = 3
TOK_DEV = 256
D = 3072
SECTIONS = 4
TOKENS = 8192
N_SECTION = 4


def raised(entries, rng, source, target, blocks, factor):
    owner, partner = [(jnp.arange(entries.shape[axis_at]) // (entries.shape[axis_at] // blocks)).reshape([-1 if axis == axis_at else 1 for axis in range(entries.ndim)]) for axis_at in (source, target)]
    chosen = jax.random.permutation(rng, blocks)[partner]
    strong = (owner == chosen) | (owner == (partner + blocks // 2) % blocks)
    return jnp.where(strong, factor * entries, entries)


def block_scale(rng, extent, split, smallest, top_value):
    factor_of = 1.0
    for dim, shards_of in split:
        heights = jax.random.uniform(jax.random.fold_in(jax.random.fold_in(rng, 6), dim), (shards_of,), jnp.float32, smallest / len(split), top_value / len(split))
        factor_of = factor_of * jnp.repeat(jnp.exp(heights), extent[dim] // shards_of).reshape((-1,) + (1,) * (len(extent) - 1 - dim))
    return factor_of


def noise(own_key, shape, scale, bound, cuts=(), dtype=jnp.bfloat16):
    result = scale * jax.random.normal(own_key, shape, jnp.float32)
    if cuts:
        result = result * block_scale(own_key, shape, cuts, -0.22, 0.18)
    return jnp.clip(result, -bound, bound).astype(dtype)


def gaussian_with(stream_key, dims, spread, most, split, heavy, held_as=jnp.bfloat16):
    entries = spread * jax.random.normal(stream_key, dims, jnp.float32)
    if split:
        entries = entries * block_scale(stream_key, dims, split, -0.22, 0.18)
    return jnp.clip(raised(entries, jax.random.fold_in(stream_key, 3), *heavy), -most, most).astype(held_as)


def setup_inputs(seed: int = 0) -> dict:
    streams_of = jax.random.split(jax.random.key(seed), 8)
    layer_in = gaussian_with(streams_of[0], (SECTIONS, TOKENS, D), 1.0, 6.0, ((0, 4), (1, 32)), (1, 2, 32, 2.75))
    norm_gain = jnp.clip(1.0 + 0.18 * jax.random.normal(streams_of[1], (SECTIONS, D), jnp.float32), 0.1, 1.9)
    conv_weight = noise(streams_of[2], (SECTIONS, CONV, D), CONV ** -0.5, 3.5, ((0, 4),), jnp.float32)
    query_weight = noise(streams_of[3], (SECTIONS, D, HEADS * FEAT), D ** -0.5, 0.109375, ((0, 4),))
    key_weight = noise(streams_of[4], (SECTIONS, D, HEADS * FEAT), D ** -0.5, 0.109375, ((0, 4),))
    out_gain = jnp.clip(1.0 + 0.18 * jax.random.normal(streams_of[5], (SECTIONS, D), jnp.float32), 0.1, 1.9)
    layer_grad = noise(streams_of[6], (SECTIONS, TOKENS, D), 1.0, 6.0, ((0, 4), (1, 32)))
    return {"layer_in": layer_in, "norm_gain": norm_gain, "conv_weight": conv_weight, "query_weight": query_weight, "key_weight": key_weight, "out_gain": out_gain, "layer_grad": layer_grad}


EPSILON = 1e-06

def to_half(values):
    return lax.optimization_barrier(values.astype(jnp.bfloat16))

def taylor_map(columns):
    feat_count = columns.shape[2]
    products = columns[:, :, :, None, :] * columns[:, :, None, :, :]
    products = products.reshape(columns.shape[0], columns.shape[1], feat_count * feat_count, columns.shape[3])
    constant = jnp.ones((columns.shape[0], columns.shape[1], 1, columns.shape[3]), jnp.float32)
    pieces = [constant, columns * feat_count ** (-0.25), products * (1.0 / math.sqrt(2.0 * feat_count))]
    return to_half(jnp.concatenate(pieces, axis=2))

def taylor_back(columns, grad_feat):
    feat_count = columns.shape[2]
    linear_part = grad_feat[:, :, 1:1 + feat_count, :]
    square_part = grad_feat[:, :, 1 + feat_count:, :].reshape(grad_feat.shape[0], grad_feat.shape[1], feat_count, feat_count, grad_feat.shape[3])
    symmetric = square_part + jnp.swapaxes(square_part, 2, 3)
    mixed_term = jnp.einsum('nhabk,nhbk->nhak', symmetric, columns, precision=lax.Precision.HIGHEST)
    return linear_part * feat_count ** (-0.25) + mixed_term * (1.0 / math.sqrt(2.0 * feat_count))

def causal_mask():
    position = jnp.arange(TOK_DEV)
    return position[:, None] >= position[None, :]

def section_forward(hidden, norm_scale, conv_taps, query_proj, key_proj, out_scale):
    total_rows = hidden.shape[0]
    blocks = total_rows // TOK_DEV
    hidden_f = hidden.astype(jnp.float32)
    inv_rms = lax.rsqrt(lax.optimization_barrier(jnp.mean(hidden_f * hidden_f, axis=1, keepdims=True)) + EPSILON)
    normed = to_half(hidden_f * inv_rms * norm_scale)
    padded = jnp.concatenate([jnp.zeros((2, D), jnp.float32), normed.astype(jnp.float32)], axis=0)
    values = to_half(conv_taps[0] * padded[:-2] + conv_taps[1] * padded[1:-1] + conv_taps[2] * padded[2:])
    queries = to_half(jnp.dot(normed, query_proj, preferred_element_type=jnp.float32))
    keys_half = to_half(jnp.dot(normed, key_proj, preferred_element_type=jnp.float32))
    query_f = queries.astype(jnp.float32).reshape(blocks, TOK_DEV, HEADS, FEAT)
    key_f = keys_half.astype(jnp.float32).reshape(blocks, TOK_DEV, HEADS, FEAT)
    value_f = values.astype(jnp.float32).reshape(blocks, TOK_DEV, HEADS, VDIM)
    query_feat = taylor_map(jnp.transpose(query_f, (0, 2, 3, 1))).astype(jnp.float32)
    key_feat = taylor_map(jnp.transpose(key_f, (0, 2, 3, 1))).astype(jnp.float32)
    scores = jnp.einsum('nbhf,nchf->nhbc', query_f, key_f) * (1.0 / math.sqrt(FEAT))
    weights = to_half(jnp.where(causal_mask(), 1.0 + scores + 0.5 * scores * scores, 0.0))
    inside = jnp.einsum('nhbc,nchv->nbhv', weights.astype(jnp.float32), value_f)
    key_state = to_half(jnp.einsum('nhtb,nbhv->nhtv', key_feat, value_f)).astype(jnp.float32)
    running = jnp.cumsum(key_state, axis=0)
    prefix = to_half(jnp.concatenate([jnp.zeros_like(key_state[:1]), running[:-1]], axis=0))
    across = jnp.einsum('nhtb,nhtv->nbhv', query_feat, prefix.astype(jnp.float32))
    numerator = (inside + across).reshape(total_rows, HEADS, VDIM)
    head_rms = lax.rsqrt(lax.optimization_barrier(jnp.mean(numerator * numerator, axis=2, keepdims=True)) + EPSILON)
    output = to_half(hidden_f + out_scale * (numerator * head_rms).reshape(total_rows, D))
    stored = (hidden_f, inv_rms, normed, query_f, key_f, value_f, weights, scores, prefix, numerator, head_rms)
    return (output, stored)

def section_backward(grad_in, stored, norm_scale, conv_taps, query_proj, key_proj, out_scale):
    hidden_f, inv_rms, normed, query_f, key_f, value_f, weights, scores, prefix, numerator, head_rms = stored
    total_rows = grad_in.shape[0]
    blocks = total_rows // TOK_DEV
    score_scale = 1.0 / math.sqrt(FEAT)
    grad_f = grad_in.astype(jnp.float32)
    grad_head = (grad_f * out_scale).reshape(total_rows, HEADS, VDIM)
    grad_numer = head_rms * grad_head - numerator * (head_rms * head_rms * head_rms) * lax.optimization_barrier(jnp.mean(grad_head * numerator, axis=2, keepdims=True))
    grad_numer_half = to_half(grad_numer).astype(jnp.float32).reshape(blocks, TOK_DEV, HEADS, VDIM)
    grad_weights = jnp.einsum('nbhv,nchv->nhbc', grad_numer_half, value_f)
    grad_scores = to_half(jnp.where(causal_mask(), grad_weights * (1.0 + scores), 0.0)).astype(jnp.float32)
    grad_query_in = jnp.einsum('nhbc,nchf->nbhf', grad_scores, key_f) * score_scale
    grad_key_in = jnp.einsum('nhbc,nbhf->nchf', grad_scores, query_f) * score_scale
    grad_value_in = jnp.einsum('nhbc,nbhv->nchv', weights.astype(jnp.float32), grad_numer_half)
    query_cols = jnp.transpose(query_f, (0, 2, 3, 1))
    key_cols = jnp.transpose(key_f, (0, 2, 3, 1))
    query_feat = taylor_map(query_cols).astype(jnp.float32)
    key_feat = taylor_map(key_cols).astype(jnp.float32)
    grad_query_feat = jnp.einsum('nbhv,nhtv->nhtb', grad_numer_half, prefix.astype(jnp.float32))
    grad_prefix = to_half(jnp.einsum('nhtb,nbhv->nhtv', query_feat, grad_numer_half)).astype(jnp.float32)
    suffix = jnp.cumsum(grad_prefix[::-1], axis=0)[::-1]
    grad_state = to_half(jnp.concatenate([suffix[1:], jnp.zeros_like(suffix[:1])], axis=0)).astype(jnp.float32)
    grad_key_feat = jnp.einsum('nbhv,nhtv->nhtb', value_f, grad_state)
    grad_value_out = jnp.einsum('nhtb,nhtv->nbhv', key_feat, grad_state)
    grad_values = (grad_value_in + grad_value_out).reshape(total_rows, D)
    grad_query = grad_query_in + jnp.transpose(taylor_back(query_cols, grad_query_feat), (0, 3, 1, 2))
    grad_key = grad_key_in + jnp.transpose(taylor_back(key_cols, grad_key_feat), (0, 3, 1, 2))
    grad_query_half = to_half(grad_query.reshape(total_rows, HEADS * FEAT))
    grad_key_half = to_half(grad_key.reshape(total_rows, HEADS * FEAT))
    contract_rows = (((1,), (1,)), ((), ()))
    grad_normed = lax.dot_general(grad_query_half, query_proj, contract_rows, preferred_element_type=jnp.float32)
    grad_normed = grad_normed + lax.dot_general(grad_key_half, key_proj, contract_rows, preferred_element_type=jnp.float32)
    padded = jnp.concatenate([grad_values, jnp.zeros((2, D), jnp.float32)], axis=0)
    grad_normed = grad_normed + (conv_taps[2] * padded[:-2] + conv_taps[1] * padded[1:-1] + conv_taps[0] * padded[2:])
    grad_scaled = grad_normed * norm_scale
    grad_hidden = inv_rms * grad_scaled - hidden_f * (inv_rms * inv_rms * inv_rms) * lax.optimization_barrier(jnp.mean(hidden_f * grad_scaled, axis=1, keepdims=True))
    return to_half(grad_f + grad_hidden)

def reference(layer_in, norm_gain, conv_weight, query_weight, key_weight, out_gain, layer_grad):
    outputs = []
    grad_list = []
    for layer_index in range(N_SECTION):
        output, stored = section_forward(layer_in[layer_index], norm_gain[layer_index], conv_weight[layer_index], query_weight[layer_index], key_weight[layer_index], out_gain[layer_index])
        grad_out = section_backward(layer_grad[layer_index], stored, norm_gain[layer_index], conv_weight[layer_index], query_weight[layer_index], key_weight[layer_index], out_gain[layer_index])
        outputs.append(output)
        grad_list.append(grad_out)
    next_input = jnp.roll(jnp.stack(outputs), 1, axis=0)
    prev_grad = jnp.roll(jnp.stack(grad_list), -1, axis=0)
    return (next_input, prev_grad)
```

```python
import functools
import math

import jax
import jax.numpy as jnp
from jax import lax
from jax.experimental import pallas as pl
from jax.experimental.pallas import tpu as pltpu
from jax.sharding import PartitionSpec as P

HEADS = 24
FEAT = 16
VDIM = 128
PACKED = 160
GROUPS = 3
GROUP_HEADS = HEADS // GROUPS
STEP_HEADS = 4
STEPS = GROUP_HEADS // STEP_HEADS
CHIPS = 16

EPSILON = 1e-06
SCORE_SCALE = 1.0 / math.sqrt(FEAT)
LINEAR_SCALE = FEAT ** (-0.25)
PAIR_SCALE = 1.0 / math.sqrt(2.0 * FEAT)

f32 = jnp.float32
bf16 = jnp.bfloat16


def dot(a, b, contract):
    return lax.dot_general(a, b, (contract, ((), ())), preferred_element_type=f32)


def kernel_params(limit_mib=40):
    return pltpu.CompilerParams(vmem_limit_bytes=limit_mib << 20)


def cost(flops, moved):
    return pl.CostEstimate(flops=flops, bytes_accessed=moved, transcendentals=0)


def rolled(block, distance):
    return pltpu.roll(block, distance % block.shape[0], 0)


def taylor_rows(cols, pair_weight):
    pieces = []
    for distance in range(FEAT // 2 + 1):
        if distance == 0:
            product = cols * cols * PAIR_SCALE
        else:
            product = cols * rolled(cols, -distance) * (PAIR_SCALE * pair_weight)
        pieces.append(product if distance < FEAT // 2 else product[: FEAT // 2])
    row = lax.broadcasted_iota(jnp.int32, (FEAT // 2, cols.shape[1]), 0)
    pieces.append(jnp.where(row == 0, 1.0, 0.0).astype(f32))
    pieces.append(cols * LINEAR_SCALE)
    return jnp.concatenate(pieces, axis=0).astype(bf16)


def taylor_back(cols, grad_rows, pair_weight):
    mixed = 2.0 * grad_rows[:FEAT] * cols
    for distance in range(1, FEAT // 2):
        part = grad_rows[FEAT * distance : FEAT * (distance + 1)]
        term = part * rolled(cols, -distance) + rolled(part * cols, distance)
        mixed = mixed + (term if pair_weight == 1.0 else pair_weight * term)
    half = FEAT // 2
    last = grad_rows[FEAT * half : FEAT * half + half]
    term = jnp.concatenate([last * cols[half:], last * cols[:half]], axis=0)
    mixed = mixed + (term if pair_weight == 1.0 else pair_weight * term)
    return grad_rows[PACKED - FEAT :] * LINEAR_SCALE + mixed * PAIR_SCALE


def project_kernel(x_ref, gain_ref, query_ref, key_ref, normed_ref, query_cols_ref, key_cols_ref):
    @pl.when(pl.program_id(0) == 0)
    def _():
        x = x_ref[...].astype(f32)
        inv_rms = lax.rsqrt(jnp.mean(x * x, axis=1, keepdims=True) + EPSILON)
        normed_ref[...] = (x * inv_rms * gain_ref[...]).astype(bf16)

    normed = normed_ref[...]
    query = dot(normed, query_ref[...], ((1,), (0,)))
    key = dot(normed, key_ref[...], ((1,), (0,)))
    query_cols_ref[...] = query.T.astype(bf16)
    key_cols_ref[...] = key.T.astype(bf16)


def project(x, gain, query_proj, key_proj):
    rows, width = x.shape
    cols = query_proj.shape[1]
    whole = lambda j: (0, 0)
    return pl.pallas_call(
        project_kernel,
        grid=(cols // 128,),
        in_specs=[
            pl.BlockSpec((rows, width), whole),
            pl.BlockSpec((1, width), whole),
            pl.BlockSpec((width, 128), lambda j: (0, j)),
            pl.BlockSpec((width, 128), lambda j: (0, j)),
        ],
        out_specs=[
            pl.BlockSpec((rows, width), whole),
            pl.BlockSpec((128, rows), lambda j: (j, 0)),
            pl.BlockSpec((128, rows), lambda j: (j, 0)),
        ],
        out_shape=[
            jax.ShapeDtypeStruct((rows, width), bf16),
            jax.ShapeDtypeStruct((cols, rows), bf16),
            jax.ShapeDtypeStruct((cols, rows), bf16),
        ],
        compiler_params=kernel_params(),
        cost_estimate=cost(4 * rows * width * cols, 8 << 20),
        name="project",
    )(x, gain, query_proj, key_proj)


def head_of(index, size):
    return slice(index * size, (index + 1) * size)


def state_kernel(normed_ref, before_ref, taps_ref, key_ref, values_ref, state_ref):
    normed = normed_ref[...].astype(f32)
    before = before_ref[...].astype(f32)
    row = lax.broadcasted_iota(jnp.int32, normed.shape, 0)
    one_back = jnp.where(row == 0, before[1:2], rolled(normed, 1))
    two_back = jnp.where(row == 0, before[0:1], rolled(one_back, 1))
    values = (taps_ref[0:1] * two_back + taps_ref[1:2] * one_back + taps_ref[2:3] * normed).astype(bf16)
    values_ref[...] = values
    for head in range(STEP_HEADS):
        feat = taylor_rows(key_ref[head_of(head, FEAT)].astype(f32), 1.0)
        state = dot(feat, values[:, head_of(head, VDIM)], ((1,), (0,)))
        state_ref[head_of(head, PACKED)] = state.astype(bf16)


def inside_kernel(query_ref, key_ref, values_ref, inside_ref):
    rows = query_ref.shape[1]
    token = lax.broadcasted_iota(jnp.int32, (rows, rows), 0)
    other = lax.broadcasted_iota(jnp.int32, (rows, rows), 1)
    for head in range(STEP_HEADS):
        query = query_ref[head_of(head, FEAT)]
        key = key_ref[head_of(head, FEAT)]
        scores = dot(query, key, ((0,), (0,))) * SCORE_SCALE
        weights = jnp.where(token >= other, 1.0 + scores + 0.5 * scores * scores, 0.0).astype(bf16)
        lanes = head_of(head, VDIM)
        inside_ref[:, lanes] = dot(weights, values_ref[:, lanes], ((1,), (0,)))


def output_kernel(query_ref, inside_ref, prefix_ref, x_ref, grad_ref, scale_ref, out_ref, numer_ref, grad_state_ref):
    for head in range(STEP_HEADS):
        lanes = head_of(head, VDIM)
        feat = taylor_rows(query_ref[head_of(head, FEAT)].astype(f32), 2.0)
        across = dot(feat, prefix_ref[head_of(head, PACKED)], ((0,), (0,)))
        numer = inside_ref[:, lanes] + across
        inv = lax.rsqrt(jnp.mean(numer * numer, axis=1, keepdims=True) + EPSILON)
        scale = scale_ref[:, lanes]
        out_ref[:, lanes] = (x_ref[:, lanes].astype(f32) + scale * (numer * inv)).astype(bf16)
        grad = grad_ref[:, lanes].astype(f32) * scale
        mean = jnp.mean(grad * numer, axis=1, keepdims=True)
        grad_numer = (inv * grad - numer * (inv * inv * inv * mean)).astype(bf16)
        numer_ref[:, lanes] = grad_numer
        grad_state_ref[head_of(head, PACKED)] = dot(feat, grad_numer, ((1,), (0,))).astype(bf16)


def inside_back_kernel(
    query_ref, key_ref, values_ref, numer_ref, prefix_ref, grad_query_ref, grad_key_ref, grad_values_ref
):
    rows = query_ref.shape[1]
    token = lax.broadcasted_iota(jnp.int32, (rows, rows), 0)
    other = lax.broadcasted_iota(jnp.int32, (rows, rows), 1)
    for head in range(STEP_HEADS):
        lanes = head_of(head, VDIM)
        query = query_ref[head_of(head, FEAT)]
        key = key_ref[head_of(head, FEAT)]
        grad_numer = numer_ref[:, lanes]
        values = values_ref[:, lanes]
        scores = dot(query, key, ((0,), (0,))) * SCORE_SCALE
        turned = dot(key, query, ((0,), (0,))) * SCORE_SCALE
        weights = jnp.where(other >= token, 1.0 + turned + 0.5 * turned * turned, 0.0).astype(bf16)
        grad_values_ref[:, lanes] = dot(weights, grad_numer, ((1,), (0,)))
        grad_weights = dot(grad_numer, values, ((1,), (1,)))
        grad_scores = jnp.where(token >= other, grad_weights * (1.0 + scores), 0.0).astype(bf16)
        grad_query = dot(key, grad_scores, ((1,), (1,))) * SCORE_SCALE
        grad_key_ref[head_of(head, FEAT)] = dot(query, grad_scores, ((1,), (0,))) * SCORE_SCALE
        grad_feat = dot(prefix_ref[head_of(head, PACKED)], grad_numer, ((1,), (1,)))
        grad_query = grad_query + taylor_back(query.astype(f32), grad_feat, 2.0)
        grad_query_ref[head_of(head, FEAT)] = grad_query.astype(bf16)


def late_kernel(key_ref, values_ref, state_ref, early_key_ref, early_values_ref, grad_key_ref, grad_values_ref):
    for head in range(STEP_HEADS):
        lanes = head_of(head, VDIM)
        key = key_ref[head_of(head, FEAT)].astype(f32)
        state = state_ref[head_of(head, PACKED)]
        grad_feat = dot(state, values_ref[:, lanes], ((1,), (1,)))
        grad_key = early_key_ref[head_of(head, FEAT)] + taylor_back(key, grad_feat, 1.0)
        grad_key_ref[head_of(head, FEAT)] = grad_key.astype(bf16)
        feat = taylor_rows(key, 1.0)
        grad_values_ref[:, lanes] = early_values_ref[:, lanes] + dot(feat, state, ((0,), (0,)))


def finish_kernel(
    grad_query_ref,
    grad_key_ref,
    query_ref,
    key_ref,
    grad_values_ref,
    after_ref,
    taps_ref,
    gain_ref,
    x_ref,
    grad_ref,
    out_ref,
):
    grad_values = grad_values_ref[...]
    after = after_ref[...]
    rows = grad_values.shape[0]
    row = lax.broadcasted_iota(jnp.int32, grad_values.shape, 0)
    one_on = jnp.where(row == rows - 1, after[0:1], rolled(grad_values, -1))
    two_on = jnp.where(row == rows - 1, after[1:2], rolled(one_on, -1))
    grad_normed = dot(grad_query_ref[...], query_ref[...], ((0,), (1,)))
    grad_normed = grad_normed + dot(grad_key_ref[...], key_ref[...], ((0,), (1,)))
    grad_normed = grad_normed + (taps_ref[2:3] * grad_values + taps_ref[1:2] * one_on + taps_ref[0:1] * two_on)
    scaled = grad_normed * gain_ref[...]
    x = x_ref[...].astype(f32)
    inv = lax.rsqrt(jnp.mean(x * x, axis=1, keepdims=True) + EPSILON)
    mean = jnp.mean(x * scaled, axis=1, keepdims=True)
    out_ref[...] = (grad_ref[...].astype(f32) + inv * scaled - x * (inv * inv * inv * mean)).astype(bf16)


def group_specs(group):
    def tokens(rows, whole):
        return pl.BlockSpec((rows, STEP_HEADS * VDIM), lambda i: (0, i + (group * STEPS if whole else 0)))

    def heads(rows, cols, whole):
        return pl.BlockSpec((STEP_HEADS * rows, cols), lambda i: (i + (group * STEPS if whole else 0), 0))

    return tokens, heads


def per_group(kernel, in_specs, out_specs, out_shape, name, flops=1 << 28):
    return pl.pallas_call(
        kernel,
        grid=(STEPS,),
        in_specs=in_specs,
        out_specs=out_specs,
        out_shape=out_shape,
        compiler_params=kernel_params(),
        cost_estimate=cost(flops, 4 << 20),
        name=name,
    )


def chip_sums_kernel(reverse, got_ref, out_ref):
    total = jnp.zeros(got_ref.shape[1:], f32)
    order = range(CHIPS - 1, -1, -1) if reverse else range(CHIPS)
    for chip in order:
        out_ref[chip] = total.astype(bf16)
        total = total + got_ref[chip].astype(f32)


def chip_sums(got, reverse):
    return pl.pallas_call(
        functools.partial(chip_sums_kernel, reverse),
        out_shape=jax.ShapeDtypeStruct(got.shape, bf16),
        compiler_params=kernel_params(16),
        cost_estimate=cost(1 << 20, 1 << 19),
        name="chip_sums",
    )(got)


def core_swap(block):
    count = lax.axis_size("seq")
    return lax.ppermute(block, "seq", [(i, i ^ 1) for i in range(count)])


def over_chips(block):
    count = lax.axis_size("seq")
    groups = [list(range(core, count, 2)) for core in range(2)]
    return lax.all_to_all(block, "seq", 0, 0, tiled=True, axis_index_groups=groups)


def add_states(one, other):
    return (one.astype(f32) + other.astype(f32)).astype(bf16)


def scan_states(state, reverse):
    core = lax.axis_index("seq") % 2
    half_rows = state.shape[0] // 2
    halves = state.reshape(2, half_rows, VDIM)
    own = lax.dynamic_index_in_dim(halves, core, 0, False)
    away = lax.dynamic_index_in_dim(halves, 1 - core, 0, False)
    other = core_swap(away)
    total = add_states(own, other)
    got = over_chips(total.reshape(CHIPS, half_rows // CHIPS, VDIM))
    before = over_chips(chip_sums(got, reverse)).reshape(half_rows, VDIM)
    behind = core == (0 if reverse else 1)
    mine = jnp.where(behind, add_states(before, other), before)
    theirs = core_swap(jnp.where(behind, before, add_states(before, own)))
    first = jnp.where(core == 0, mine, theirs)
    second = jnp.where(core == 0, theirs, mine)
    return jnp.concatenate([first, second], axis=0)


def neighbour_rows(edge, distance):
    devices = range(lax.axis_size("seq"))
    route = [(i - distance, i) for i in devices if i - distance in devices]
    return lax.ppermute(edge, "seq", route)


def section_pass(block, distance):
    count = lax.axis_size("section")
    return lax.ppermute(block, "section", [((i - distance) % count, i) for i in range(count)])


def section_pass_cut(block, distance, pieces):
    rows = block.shape[0] // pieces
    return jnp.concatenate(
        [section_pass(block[k * rows : (k + 1) * rows], distance) for k in range(pieces)], axis=0
    )


def local(layer_in, norm_gain, conv_weight, query_weight, key_weight, out_gain, layer_grad):
    x, grad = layer_in[0], layer_grad[0]
    taps, query_proj, key_proj = conv_weight[0], query_weight[0], key_weight[0]
    rows, width = x.shape
    group_width = GROUP_HEADS * VDIM
    shape = jax.ShapeDtypeStruct

    normed, query, key = project(x, norm_gain, query_proj, key_proj)
    before = neighbour_rows(normed[-2:], 1)

    values, prefixes = [], []
    for group in range(GROUPS):
        tokens, heads = group_specs(group)
        value, state = per_group(
            state_kernel,
            [tokens(rows, True), tokens(2, True), tokens(3, True), heads(FEAT, rows, True)],
            [tokens(rows, False), heads(PACKED, VDIM, False)],
            [shape((rows, group_width), bf16), shape((GROUP_HEADS * PACKED, VDIM), bf16)],
            "state",
        )(normed, before, taps, key)
        values.append(value)
        prefixes.append(scan_states(state, False))

    insides = []
    for group in range(GROUPS):
        tokens, heads = group_specs(group)
        insides.append(
            per_group(
                inside_kernel,
                [heads(FEAT, rows, True), heads(FEAT, rows, True), tokens(rows, False)],
                tokens(rows, False),
                shape((rows, group_width), f32),
                "inside",
            )(query, key, values[group])
        )

    outputs, grad_numers, grad_states = [], [], []
    for group in range(GROUPS):
        tokens, heads = group_specs(group)
        output, grad_numer, grad_prefix = per_group(
            output_kernel,
            [
                heads(FEAT, rows, True),
                tokens(rows, False),
                heads(PACKED, VDIM, False),
                tokens(rows, True),
                tokens(rows, True),
                tokens(1, True),
            ],
            [tokens(rows, False), tokens(rows, False), heads(PACKED, VDIM, False)],
            [
                shape((rows, group_width), bf16),
                shape((rows, group_width), bf16),
                shape((GROUP_HEADS * PACKED, VDIM), bf16),
            ],
            "output",
        )(query, insides[group], prefixes[group], x, grad, out_gain)
        outputs.append(output)
        grad_numers.append(grad_numer)
        grad_states.append(scan_states(grad_prefix, True))
    sent_forward = section_pass(jnp.concatenate(outputs, axis=1), 1)

    grad_queries, grad_keys, grad_values = [], [], []
    for group in range(GROUPS):
        tokens, heads = group_specs(group)
        grad_query, grad_key, grad_value = per_group(
            inside_back_kernel,
            [
                heads(FEAT, rows, True),
                heads(FEAT, rows, True),
                tokens(rows, False),
                tokens(rows, False),
                heads(PACKED, VDIM, False),
            ],
            [heads(FEAT, rows, False), heads(FEAT, rows, False), tokens(rows, False)],
            [
                shape((GROUP_HEADS * FEAT, rows), bf16),
                shape((GROUP_HEADS * FEAT, rows), f32),
                shape((rows, group_width), f32),
            ],
            "inside_back",
        )(query, key, values[group], grad_numers[group], prefixes[group])
        grad_queries.append(grad_query)
        grad_keys.append(grad_key)
        grad_values.append(grad_value)

    for group in range(GROUPS):
        tokens, heads = group_specs(group)
        grad_keys[group], grad_values[group] = per_group(
            late_kernel,
            [
                heads(FEAT, rows, True),
                tokens(rows, False),
                heads(PACKED, VDIM, False),
                heads(FEAT, rows, False),
                tokens(rows, False),
            ],
            [heads(FEAT, rows, False), tokens(rows, False)],
            [shape((GROUP_HEADS * FEAT, rows), bf16), shape((rows, group_width), f32)],
            "late",
        )(key, values[group], grad_states[group], grad_keys[group], grad_values[group])
    grad_query = jnp.concatenate(grad_queries, axis=0)
    grad_key = jnp.concatenate(grad_keys, axis=0)
    grad_value = jnp.concatenate(grad_values, axis=1)
    after = neighbour_rows(grad_value[:2], -1)
    in_grad = pl.pallas_call(
        finish_kernel,
        out_shape=shape((rows, width), bf16),
        compiler_params=kernel_params(),
        cost_estimate=cost(4 * rows * width * query_proj.shape[1], 16 << 20),
        name="finish",
    )(grad_query, grad_key, query_proj, key_proj, grad_value, after, taps, norm_gain, x, grad)
    sent_backward = section_pass_cut(in_grad, -1, 4)
    return (sent_forward[None], sent_backward[None])


def solution(mesh):
    return jax.shard_map(
        local,
        mesh=mesh,
        in_specs=(
            P("section", "seq", None),
            P("section", None),
            P("section", None, None),
            P("section", None, None),
            P("section", None, None),
            P("section", None),
            P("section", "seq", None),
        ),
        out_specs=(P("section", "seq", None), P("section", "seq", None)),
        check_vma=False,
    )
```

```python
import functools
import math

import jax
import jax.numpy as jnp
from jax import lax
from jax.experimental import pallas as pl
from jax.experimental.pallas import tpu as pltpu
from jax.sharding import PartitionSpec as P

HEADS = 24
FEAT = 16
VDIM = 128
PACKED = 160
HALF = HEADS // 2
STEP_HEADS = 4
STEPS = HEADS // STEP_HEADS
STEP_LANES = STEP_HEADS * VDIM
HALF_STATE = HALF * PACKED
CHIPS = 16
PIECES = 4

EPSILON = 1e-06
SCORE_SCALE = 1.0 / math.sqrt(FEAT)
LINEAR_SCALE = FEAT ** (-0.25)
PAIR_SCALE = 1.0 / math.sqrt(2.0 * FEAT)

f32 = jnp.float32
bf16 = jnp.bfloat16


def dot(a, b, contract):
    return lax.dot_general(a, b, (contract, ((), ())), preferred_element_type=f32)


IN_HBM = pl.BlockSpec(memory_space=pltpu.HBM)
IN_SMEM = pl.BlockSpec(memory_space=pltpu.SMEM)


def params(micros, limit_mib=16):
    return dict(
        compiler_params=pltpu.CompilerParams(vmem_limit_bytes=limit_mib << 20),
        cost_estimate=pl.CostEstimate(flops=int(micros * 1.1e9), bytes_accessed=1 << 16, transcendentals=0),
    )


def shaped(*shapes):
    return [jax.ShapeDtypeStruct(dims, dtype) for dims, dtype in shapes]


def streamed(kernel, operands, out_shape, name, micros, scratch, copies, in_specs=None, limit_mib=62):
    return pl.pallas_call(
        kernel,
        in_specs=in_specs or [IN_HBM] * len(operands),
        out_specs=[IN_HBM] * len(out_shape),
        out_shape=shaped(*out_shape),
        scratch_shapes=[pltpu.VMEM(dims, dtype) for dims, dtype in scratch] + [pltpu.SemaphoreType.DMA((copies,))],
        name=name,
        **params(micros, limit_mib),
    )(*operands)


class Copies:
    def __init__(self, sems):
        self.sems, self.used = sems, 0

    def start(self, source, target):
        copy = pltpu.make_async_copy(source, target, self.sems.at[self.used])
        self.used += 1
        copy.start()
        return copy


def wait_all(copies):
    for copy in copies:
        copy.wait()


def rolled(block, distance):
    return pltpu.roll(block, distance % block.shape[0], 0)


def taylor_rows(cols, pair_weight):
    pieces = []
    for distance in range(FEAT // 2 + 1):
        if distance == 0:
            product = cols * cols * PAIR_SCALE
        else:
            product = cols * rolled(cols, -distance) * (PAIR_SCALE * pair_weight)
        pieces.append(product if distance < FEAT // 2 else product[: FEAT // 2])
    row = lax.broadcasted_iota(jnp.int32, (FEAT // 2, cols.shape[1]), 0)
    pieces.append(jnp.where(row == 0, 1.0, 0.0).astype(f32))
    pieces.append(cols * LINEAR_SCALE)
    return jnp.concatenate(pieces, axis=0).astype(bf16)


def taylor_back(cols, grad_rows, pair_weight):
    mixed = 2.0 * grad_rows[:FEAT] * cols
    for distance in range(1, FEAT // 2):
        part = grad_rows[FEAT * distance : FEAT * (distance + 1)]
        term = part * rolled(cols, -distance) + rolled(part * cols, distance)
        mixed = mixed + (term if pair_weight == 1.0 else pair_weight * term)
    half = FEAT // 2
    last = grad_rows[FEAT * half : FEAT * half + half]
    term = jnp.concatenate([last * cols[half:], last * cols[:half]], axis=0)
    mixed = mixed + (term if pair_weight == 1.0 else pair_weight * term)
    return grad_rows[PACKED - FEAT :] * LINEAR_SCALE + mixed * PAIR_SCALE


def head_of(index, size):
    return slice(index * size, (index + 1) * size)


def lanes_of(step):
    return slice(step * STEP_LANES, (step + 1) * STEP_LANES)


def half_rows(half):
    return pl.ds(pl.multiple_of(half * HALF_STATE, HALF_STATE), HALF_STATE)


def by_lanes(copies, source, target, steps=range(STEPS)):
    return [copies.start(source.at[:, lanes_of(step)], target.at[:, lanes_of(step)]) for step in steps]


def edge_kernel(x_hbm, gain_hbm, out_hbm, x_ref, gain_ref, out_ref, sems):
    copies = Copies(sems)
    rows = x_hbm.shape[0]
    wait_all([copies.start(x_hbm.at[rows - 16 : rows], x_ref), copies.start(gain_hbm, gain_ref)])
    x = x_ref[...].astype(f32)
    inv_rms = lax.rsqrt(jnp.mean(x * x, axis=1, keepdims=True) + EPSILON)
    out_ref[...] = (x * inv_rms * gain_ref[...]).astype(bf16)
    copies.start(out_ref, out_hbm).wait()


def edge_rows(x, gain):
    width = x.shape[1]
    edge = ((16, width), bf16)
    return streamed(edge_kernel, [x, gain], [edge], "edge", 1, [edge, ((1, width), f32), edge], 3)[0]


def state_kernel(
    core_ref,
    x_hbm,
    gain_hbm,
    query_hbm,
    key_hbm,
    before_hbm,
    taps_hbm,
    values_hbm,
    cols_hbm,
    own_hbm,
    away_hbm,
    x_ref,
    gain_ref,
    weight_ref,
    before_ref,
    taps_ref,
    normed_ref,
    values_ref,
    cols_ref,
    state_ref,
    sems,
):
    copies = Copies(sems)
    middle = query_hbm.shape[1]
    rows = x_ref.shape[0]
    first = [copies.start(x_hbm, x_ref), copies.start(gain_hbm, gain_ref)]
    weights = [
        copies.start(query_hbm, weight_ref.at[:, :middle]),
        copies.start(key_hbm, weight_ref.at[:, middle:]),
        copies.start(before_hbm, before_ref),
        copies.start(taps_hbm, taps_ref),
    ]
    wait_all(first)

    @pl.loop(0, rows // 16)
    def _(step):
        here = pl.ds(pl.multiple_of(step * 16, 16), 16)
        x = x_ref[here].astype(f32)
        inv_rms = lax.rsqrt(jnp.mean(x * x, axis=1, keepdims=True) + EPSILON)
        normed_ref[here] = (x * inv_rms * gain_ref[...]).astype(bf16)

    wait_all(weights)
    cols_ref[...] = dot(normed_ref[...], weight_ref[...], ((1,), (0,))).T.astype(bf16)
    out = [copies.start(cols_ref, cols_hbm)]
    edge = before_ref.shape[0]
    for step in range(STEPS):
        lanes = lanes_of(step)
        normed = normed_ref[:, lanes].astype(f32)
        before = before_ref[:, lanes].astype(f32)[edge - 8 :]
        row = lax.broadcasted_iota(jnp.int32, normed.shape, 0)
        one_back = jnp.where(row == 0, before[7:8], rolled(normed, 1))
        two_back = jnp.where(row == 0, before[6:7], rolled(one_back, 1))
        taps = taps_ref[:, lanes]
        values = (taps[0:1] * two_back + taps[1:2] * one_back + taps[2:3] * normed).astype(bf16)
        values_ref[:, lanes] = values
        out += by_lanes(copies, values_ref, values_hbm, [step])
        for head in range(STEP_HEADS):
            place = step * STEP_HEADS + head
            keys = cols_ref[middle + place * FEAT : middle + (place + 1) * FEAT].astype(f32)
            state = dot(taylor_rows(keys, 1.0), values[:, head_of(head, VDIM)], ((1,), (0,)))
            state_ref[head_of(place, PACKED)] = state.astype(bf16)
    core = core_ref[0]
    out.append(copies.start(state_ref.at[half_rows(1 - core)], away_hbm))
    out.append(copies.start(state_ref.at[half_rows(core)], own_hbm))
    wait_all(out)


def causal(rows):
    token = lax.broadcasted_iota(jnp.int32, (rows, rows), 0)
    other = lax.broadcasted_iota(jnp.int32, (rows, rows), 1)
    return token >= other, other >= token


def half_lanes(half):
    return slice(half * HALF * VDIM, (half + 1) * HALF * VDIM)


def inside_kernel(half, cols_hbm, values_hbm, inside_hbm, cols_ref, values_ref, inside_ref, sems):
    copies = Copies(sems)
    first = copies.start(cols_hbm, cols_ref)
    here = half_lanes(half)
    blocks = by_lanes(copies, values_hbm.at[:, here], values_ref, range(STEPS // 2))
    first.wait()
    middle, rows = cols_ref.shape[0] // 2, cols_ref.shape[1]
    mask, _ = causal(rows)
    out = []
    for step in range(STEPS // 2):
        blocks[step].wait()
        for head in range(STEP_HEADS):
            place = half * HALF + step * STEP_HEADS + head
            query = cols_ref[head_of(place, FEAT)]
            key = cols_ref[middle + place * FEAT : middle + (place + 1) * FEAT]
            scores = dot(query, key, ((0,), (0,))) * SCORE_SCALE
            weights = jnp.where(mask, 1.0 + scores + 0.5 * scores * scores, 0.0).astype(bf16)
            lanes = head_of(step * STEP_HEADS + head, VDIM)
            inside_ref[:, lanes] = dot(weights, values_ref[:, lanes], ((1,), (0,))).astype(bf16)
        out += by_lanes(copies, inside_ref, inside_hbm, [step])
    wait_all(out)


def states_in(copies, core, before_hbm, other_hbm, theirs_hbm, state_ref, other_ref):
    return [
        copies.start(before_hbm, state_ref.at[half_rows(core)]),
        copies.start(other_hbm, other_ref),
        copies.start(theirs_hbm, state_ref.at[half_rows(1 - core)]),
    ]


def state_of(place, adds_other, state_ref, other_ref):
    half, within = place // HALF, place % HALF
    state = state_ref[head_of(place, PACKED)]
    both = add_states(state, other_ref[head_of(within, PACKED)])
    return jnp.where(adds_other[half], both, state)


def head_mean(terms, ones):
    return dot(terms.astype(bf16), ones, ((1,), (0,))) * (1.0 / VDIM)


def output_kernel(
    core_ref,
    cols_hbm,
    inside_low_hbm,
    inside_high_hbm,
    before_hbm,
    other_hbm,
    theirs_hbm,
    x_hbm,
    grad_hbm,
    scale_hbm,
    out_hbm,
    numer_hbm,
    prefix_hbm,
    grad_own_hbm,
    grad_away_hbm,
    cols_ref,
    inside_ref,
    prefix_ref,
    other_ref,
    x_ref,
    grad_ref,
    scale_ref,
    out_ref,
    numer_ref,
    state_ref,
    sems,
):
    copies = Copies(sems)
    core = core_ref[0]
    middle = cols_ref.shape[0] // 2
    first = states_in(copies, core, before_hbm, other_hbm, theirs_hbm, prefix_ref, other_ref)
    first += [copies.start(cols_hbm.at[:middle], cols_ref.at[:middle]), copies.start(scale_hbm, scale_ref)]
    blocks = []
    for step in range(STEPS):
        source = inside_low_hbm if step < STEPS // 2 else inside_high_hbm
        blocks.append(
            [copies.start(source.at[:, lanes_of(step % (STEPS // 2))], inside_ref.at[:, lanes_of(step)])]
            + by_lanes(copies, x_hbm, x_ref, [step])
            + by_lanes(copies, grad_hbm, grad_ref, [step])
        )
    wait_all(first)
    adds_other = (False, core == 1)
    ones = jnp.ones((VDIM, VDIM), bf16)
    out = []
    for step in range(STEPS):
        wait_all(blocks[step])
        for head in range(STEP_HEADS):
            place = step * STEP_HEADS + head
            lanes = head_of(place, VDIM)
            feat = taylor_rows(cols_ref[head_of(place, FEAT)].astype(f32), 2.0)
            prefix = state_of(place, adds_other, prefix_ref, other_ref)
            prefix_ref[head_of(place, PACKED)] = prefix
            numer = inside_ref[:, lanes].astype(f32) + dot(feat, prefix, ((0,), (0,)))
            scale = scale_ref[:, lanes]
            grad = grad_ref[:, lanes].astype(f32) * scale
            inv = lax.rsqrt(head_mean(numer * numer, ones) + EPSILON)
            mean = head_mean(grad * numer, ones)
            out_ref[:, lanes] = (x_ref[:, lanes].astype(f32) + scale * (numer * inv)).astype(bf16)
            grad_numer = (inv * grad - numer * (inv * inv * inv * mean)).astype(bf16)
            numer_ref[:, lanes] = grad_numer
            state_ref[head_of(place, PACKED)] = dot(feat, grad_numer, ((1,), (0,))).astype(bf16)
        out += by_lanes(copies, out_ref, out_hbm, [step]) + by_lanes(copies, numer_ref, numer_hbm, [step])
    out.append(copies.start(state_ref.at[half_rows(1 - core)], grad_away_hbm))
    out.append(copies.start(state_ref.at[half_rows(core)], grad_own_hbm))
    out.append(copies.start(prefix_ref, prefix_hbm))
    wait_all(out)


def inside_back_kernel(
    half,
    cols_hbm,
    values_hbm,
    numer_hbm,
    prefix_hbm,
    grad_cols_hbm,
    grad_values_hbm,
    cols_ref,
    values_ref,
    numer_ref,
    prefix_ref,
    grad_cols_ref,
    grad_values_ref,
    sems,
):
    copies = Copies(sems)
    here = half_lanes(half)
    steps = range(STEPS // 2)
    first = [copies.start(cols_hbm, cols_ref)]
    state_rows = slice(half * HALF_STATE, (half + 1) * HALF_STATE)
    blocks = [
        by_lanes(copies, numer_hbm.at[:, here], numer_ref, [step])
        + by_lanes(copies, values_hbm.at[:, here], values_ref, [step])
        for step in steps
    ]
    first.append(copies.start(prefix_hbm.at[state_rows], prefix_ref))
    wait_all(first)
    middle, rows = cols_ref.shape[0] // 2, cols_ref.shape[1]
    mask, turned_mask = causal(rows)
    out = []
    for step in steps:
        wait_all(blocks[step])
        for head in range(STEP_HEADS):
            within = step * STEP_HEADS + head
            place = half * HALF + within
            lanes = head_of(within, VDIM)
            query = cols_ref[head_of(place, FEAT)]
            key = cols_ref[middle + place * FEAT : middle + (place + 1) * FEAT]
            grad_numer, values = numer_ref[:, lanes], values_ref[:, lanes]
            scores = dot(query, key, ((0,), (0,))) * SCORE_SCALE
            turned = dot(key, query, ((0,), (0,))) * SCORE_SCALE
            weights = jnp.where(turned_mask, 1.0 + turned + 0.5 * turned * turned, 0.0).astype(bf16)
            grad_values_ref[:, lanes] = dot(weights, grad_numer, ((1,), (0,))).astype(bf16)
            grad_weights = dot(grad_numer, values, ((1,), (1,)))
            grad_scores = jnp.where(mask, grad_weights * (1.0 + scores), 0.0).astype(bf16)
            grad_query = dot(key, grad_scores, ((1,), (1,))) * SCORE_SCALE
            grad_key = dot(query, grad_scores, ((1,), (0,))) * SCORE_SCALE
            grad_feat = dot(prefix_ref[head_of(within, PACKED)], grad_numer, ((1,), (1,)))
            grad_cols_ref[head_of(within, FEAT)] = grad_query + taylor_back(query.astype(f32), grad_feat, 2.0)
            grad_cols_ref[head_of(HALF + within, FEAT)] = grad_key
        out += by_lanes(copies, grad_values_ref, grad_values_hbm, [step])
    out.append(copies.start(grad_cols_ref, grad_cols_hbm))
    wait_all(out)


def late_kernel(
    core_ref,
    cols_hbm,
    values_hbm,
    before_hbm,
    other_hbm,
    theirs_hbm,
    cols_low_hbm,
    cols_high_hbm,
    values_low_hbm,
    values_high_hbm,
    query_hbm,
    key_hbm,
    taps_hbm,
    gain_hbm,
    x_hbm,
    grad_hbm,
    forward_hbm,
    *rest,
):
    edge_hbm, scaled_hbm, sums_hbm, forward_out_hbm = rest[:4]
    piece_hbms, rest = rest[4 : 3 + PIECES], rest[3 + PIECES :]
    (
        cols_ref,
        values_ref,
        state_ref,
        other_ref,
        grads_ref,
        early_ref,
        query_ref,
        key_ref,
        taps_ref,
        gain_ref,
        x_ref,
        grad_ref,
        grad_values_ref,
        turned_ref,
        scaled_ref,
        sums_ref,
        out_ref,
        edge_ref,
        forward_ref,
        sems,
    ) = rest
    copies = Copies(sems)
    core = core_ref[0]
    middle, rows = cols_ref.shape[0], cols_ref.shape[1]
    half_cols = middle // 2
    first = states_in(copies, core, before_hbm, other_hbm, theirs_hbm, state_ref, other_ref)
    first.append(copies.start(cols_hbm.at[middle:], cols_ref))
    for half, source in enumerate((cols_low_hbm, cols_high_hbm)):
        for kind in range(2):
            start = kind * middle + half * half_cols
            first.append(
                copies.start(
                    source.at[kind * half_cols : (kind + 1) * half_cols], grads_ref.at[start : start + half_cols]
                )
            )
    blocks = []
    for step in range(STEPS):
        source = values_low_hbm if step < STEPS // 2 else values_high_hbm
        blocks.append(
            by_lanes(copies, values_hbm, values_ref, [step])
            + [copies.start(source.at[:, lanes_of(step % (STEPS // 2))], early_ref.at[:, lanes_of(step)])]
        )
    weights = [copies.start(taps_hbm, taps_ref), copies.start(gain_hbm, gain_ref)]
    for step in range(STEPS):
        lanes = lanes_of(step)
        weights.append(copies.start(query_hbm.at[lanes], query_ref.at[lanes]))
        weights.append(copies.start(key_hbm.at[lanes], key_ref.at[lanes]))
    weights += [copies.start(x_hbm, x_ref), copies.start(grad_hbm, grad_ref)]
    forward_in = copies.start(forward_hbm, forward_ref)
    wait_all(first)
    adds_other = (core == 0, False)
    for step in range(STEPS):
        wait_all(blocks[step])
        for head in range(STEP_HEADS):
            place = step * STEP_HEADS + head
            lanes = head_of(place, VDIM)
            key = cols_ref[head_of(place, FEAT)].astype(f32)
            state = state_of(place, adds_other, state_ref, other_ref)
            grad_feat = dot(state, values_ref[:, lanes], ((1,), (1,)))
            key_rows = slice(middle + place * FEAT, middle + (place + 1) * FEAT)
            grads_ref[key_rows] = grads_ref[key_rows] + taylor_back(key, grad_feat, 1.0)
            late = dot(taylor_rows(key, 1.0), state, ((0,), (0,)))
            grad_values_ref[:, lanes] = early_ref[:, lanes].astype(f32) + late
    edge_ref[...] = grad_values_ref[:8]
    forward_in.wait()
    out = [copies.start(forward_ref, forward_out_hbm), copies.start(edge_ref, edge_hbm)]
    turned_ref[...] = grads_ref[...].T.astype(bf16)
    wait_all(weights)
    total = jnp.zeros((rows, VDIM), f32)
    squares = jnp.zeros((rows, VDIM), f32)
    for step in range(STEPS):
        lanes = lanes_of(step)
        grad_values = grad_values_ref[:, lanes]
        row = lax.broadcasted_iota(jnp.int32, grad_values.shape, 0)
        one_on = jnp.where(row == rows - 1, 0.0, rolled(grad_values, -1))
        two_on = jnp.where(row == rows - 1, 0.0, rolled(one_on, -1))
        grad_normed = dot(turned_ref[:, :middle], query_ref[lanes], ((1,), (1,)))
        grad_normed = grad_normed + dot(turned_ref[:, middle:], key_ref[lanes], ((1,), (1,)))
        taps = taps_ref[:, lanes]
        grad_normed = grad_normed + (taps[2:3] * grad_values + taps[1:2] * one_on + taps[0:1] * two_on)
        scaled = grad_normed * gain_ref[:, lanes]
        scaled_ref[:, lanes] = scaled
        x = x_ref[:, lanes].astype(f32)
        for head in range(STEP_HEADS):
            x_part, scaled_part = x[:, head_of(head, VDIM)], scaled[:, head_of(head, VDIM)]
            total = total + x_part * scaled_part
            squares = squares + x_part * x_part
    total = jnp.sum(total, axis=1, keepdims=True)
    squares = jnp.sum(squares, axis=1, keepdims=True)
    lane = lax.broadcasted_iota(jnp.int32, (rows, VDIM), 1)
    sums_ref[...] = jnp.where(lane == 0, total, jnp.where(lane == 1, squares, 0.0))
    cut = rows // PIECES
    tail = slice(rows - cut, rows)
    out += [copies.start(scaled_ref.at[tail], scaled_hbm), copies.start(sums_ref.at[tail], sums_hbm)]
    for piece in range(PIECES - 1):
        here = slice(piece * cut, (piece + 1) * cut)
        out_ref[here] = input_grad(scaled_ref[here], sums_ref[here], x_ref[here], grad_ref[here])
        out.append(copies.start(out_ref.at[here], piece_hbms[piece]))
    wait_all(out)


def input_grad(scaled, sums, x, grad):
    width = x.shape[1]
    inv = lax.rsqrt(sums[:, 1:2] / width + EPSILON)
    pull = inv * inv * inv * (sums[:, 0:1] / width)
    return (grad.astype(f32) + inv * scaled - x.astype(f32) * pull).astype(bf16)


def last_kernel(scaled_ref, sums_ref, x_ref, grad_ref, after_ref, taps_ref, gain_ref, out_ref):
    rows, width = x_ref.shape
    after = after_ref[...]
    row = lax.broadcasted_iota(jnp.int32, (rows, width), 0)
    upper = taps_ref[0:1] * after[0:1]
    lower = taps_ref[1:2] * after[0:1] + taps_ref[0:1] * after[1:2]
    extra = jnp.where(row == rows - 2, upper, jnp.where(row == rows - 1, lower, 0.0)) * gain_ref[...]
    with_x = jnp.sum(x_ref[...].astype(f32) * extra, axis=1, keepdims=True)
    lane = lax.broadcasted_iota(jnp.int32, sums_ref.shape, 1)
    sums = sums_ref[...] + jnp.where(lane == 0, with_x, 0.0)
    out_ref[...] = input_grad(scaled_ref[...] + extra, sums, x_ref[...], grad_ref[...])


def chip_sums_kernel(reverse, got_ref, out_ref):
    total = jnp.zeros(got_ref.shape[1:], f32)
    order = range(CHIPS - 1, -1, -1) if reverse else range(CHIPS)
    for chip in order:
        out_ref[chip] = total.astype(bf16)
        total = total + got_ref[chip].astype(f32)


def chip_sums(got, reverse):
    return pl.pallas_call(
        functools.partial(chip_sums_kernel, reverse),
        out_shape=jax.ShapeDtypeStruct(got.shape, bf16),
        name="chip_sums",
        **params(0.8),
    )(got)


def pair_sum_kernel(own_ref, other_ref, out_ref):
    rows = out_ref.shape[1]
    for chip in range(CHIPS):
        here = head_of(chip, rows)
        out_ref[chip] = add_states(own_ref[here], other_ref[here])


def pair_sum(own, other):
    return pl.pallas_call(
        pair_sum_kernel,
        out_shape=jax.ShapeDtypeStruct((CHIPS, own.shape[0] // CHIPS, VDIM), bf16),
        name="pair_sum",
        **params(0.5),
    )(own, other)


def join_kernel(*refs):
    *pieces, out_hbm, sems = refs
    copies = Copies(sems)
    rows = pieces[0].shape[0]
    wait_all([copies.start(piece, out_hbm.at[head_of(k, rows)]) for k, piece in enumerate(pieces)])


def joined(pieces):
    rows, width = pieces[0].shape
    anywhere = pl.BlockSpec(memory_space=pl.ANY)
    return pl.pallas_call(
        join_kernel,
        in_specs=[anywhere] * len(pieces),
        out_specs=anywhere,
        out_shape=jax.ShapeDtypeStruct((rows * len(pieces), width), bf16),
        scratch_shapes=[pltpu.SemaphoreType.DMA((len(pieces),))],
        name="join",
        **params(1),
    )(*pieces)


def core_swap(block):
    count = lax.axis_size("seq")
    return lax.ppermute(block, "seq", [(i, i ^ 1) for i in range(count)])


def over_chips(block):
    count = lax.axis_size("seq")
    groups = [list(range(core, count, 2)) for core in range(2)]
    return lax.all_to_all(block, "seq", 0, 0, tiled=True, axis_index_groups=groups)


def add_states(one, other):
    return (one.astype(f32) + other.astype(f32)).astype(bf16)


def scan_first(away, own):
    other = core_swap(away)
    return over_chips(pair_sum(own, other)), other


def scan_second(before, own, counts_own):
    before = before.reshape(own.shape)
    theirs = core_swap(jnp.where(counts_own, add_states(before, own), before))
    return before, theirs


def neighbour_rows(edge, distance):
    devices = range(lax.axis_size("seq"))
    route = [(i - distance, i) for i in devices if i - distance in devices]
    return lax.ppermute(edge, "seq", route)


def section_pass(block, distance):
    count = lax.axis_size("section")
    return lax.ppermute(block, "section", [((i - distance) % count, i) for i in range(count)])


def local(layer_in, norm_gain, conv_weight, query_weight, key_weight, out_gain, layer_grad):
    x, grad = layer_in[0], layer_grad[0]
    taps, query_proj, key_proj = conv_weight[0], query_weight[0], key_weight[0]
    rows, width = x.shape
    both = 2 * query_proj.shape[1]
    half_width = width // 2
    cut = rows // PIECES
    parity = lax.axis_index("seq") % 2
    core = parity.reshape(1).astype(jnp.int32)
    half_state = ((HALF_STATE, VDIM), bf16)
    all_state = ((2 * HALF_STATE, VDIM), bf16)
    tokens, tokens_wide = ((rows, width), bf16), ((rows, width), f32)
    cols_shape = ((both, rows), bf16)

    before_edge = neighbour_rows(edge_rows(x, norm_gain), 1)
    values, cols, own, away = streamed(
        state_kernel,
        [core, x, norm_gain, query_proj, key_proj, before_edge, taps],
        [tokens, cols_shape, half_state, half_state],
        "state",
        8,
        [tokens, ((1, width), f32), ((width, both), bf16), ((16, width), bf16), ((3, width), f32)]
        + [tokens, tokens, cols_shape, all_state],
        6 + 3 + STEPS,
        in_specs=[IN_SMEM] + [IN_HBM] * 6,
    )

    def inside(half, cols, values):
        shape = ((rows, half_width), bf16)
        return streamed(
            functools.partial(inside_kernel, half),
            [cols, values],
            [shape],
            "inside",
            3,
            [cols_shape, shape, shape],
            1 + STEPS,
        )[0]

    got, other = scan_first(away, own)
    got, inside_low = lax.optimization_barrier((got, inside(0, cols, values)))
    _, values_then = lax.optimization_barrier((got, values))
    before, inside_high = lax.optimization_barrier((over_chips(chip_sums(got, False)), inside(1, cols, values_then)))
    before, theirs = scan_second(before, own, parity == 0)
    output, numer, prefix, grad_own, grad_away = streamed(
        output_kernel,
        [core, cols, inside_low, inside_high, before, other, theirs, x, grad, out_gain],
        [tokens, tokens, all_state, half_state, half_state],
        "output",
        8,
        [cols_shape, tokens, all_state, half_state, tokens, tokens, ((1, width), f32), tokens, tokens, all_state],
        5 + 3 * STEPS + 2 * STEPS + 3,
        in_specs=[IN_SMEM] + [IN_HBM] * 9,
    )
    sent_forward = section_pass(output, 1)

    def inside_back(half, numer):
        shape = ((rows, half_width), bf16)
        grads = ((both // 2, rows), f32)
        return streamed(
            functools.partial(inside_back_kernel, half),
            [cols, values, numer, prefix],
            [grads, shape],
            "inside_back",
            5,
            [cols_shape, shape, shape, half_state, grads, shape],
            2 + 3 * (STEPS // 2) + 1,
        )

    got, grad_other = scan_first(grad_away, grad_own)
    got, low = lax.optimization_barrier((got, inside_back(0, numer)))
    _, numer_then = lax.optimization_barrier((got, numer))
    grad_before, high = lax.optimization_barrier((over_chips(chip_sums(got, True)), inside_back(1, numer_then)))
    grad_before, grad_theirs = scan_second(grad_before, grad_own, parity == 1)
    edge, scaled, sums, sent_forward, *pieces = streamed(
        late_kernel,
        [core, cols, values, grad_before, grad_other, grad_theirs, low[0], high[0], low[1], high[1]]
        + [query_proj, key_proj, taps, norm_gain, x, grad, sent_forward],
        [((8, width), f32), ((cut, width), f32), ((cut, VDIM), f32), tokens] + [((cut, width), bf16)] * (PIECES - 1),
        "late",
        9,
        [((both // 2, rows), bf16), tokens, all_state, half_state, ((both, rows), f32), tokens]
        + [((width, both // 2), bf16)] * 2
        + [((3, width), f32), ((1, width), f32), tokens, tokens, tokens_wide, ((rows, both), bf16), tokens_wide]
        + [((rows, VDIM), f32), tokens, ((8, width), f32), tokens],
        3 + 1 + 4 + 2 * STEPS + 2 + 2 * STEPS + 2 + 3 + 2 + PIECES - 1,
        in_specs=[IN_SMEM] + [IN_HBM] * 16,
    )
    after_edge = neighbour_rows(edge, -1)
    at_last = lambda: pl.BlockSpec((cut, width), lambda i: (PIECES - 1, 0))
    whole = lambda n, cols=width: pl.BlockSpec((n, cols), lambda i: (0, 0))
    pieces.append(
        pl.pallas_call(
            last_kernel,
            grid=(1,),
            in_specs=[whole(cut), whole(cut, VDIM), at_last(), at_last(), whole(8), whole(3), whole(1)],
            out_specs=whole(cut),
            out_shape=jax.ShapeDtypeStruct((cut, width), bf16),
            name="last",
            **params(1),
        )(scaled, sums, x, grad, after_edge, taps, norm_gain)
    )
    sent_backward = joined([section_pass(piece, -1) for piece in pieces])
    return (sent_forward[None], sent_backward[None])


def solution(mesh):
    return jax.shard_map(
        local,
        mesh=mesh,
        in_specs=(
            P("section", "seq", None),
            P("section", None),
            P("section", None, None),
            P("section", None, None),
            P("section", None, None),
            P("section", None),
            P("section", "seq", None),
        ),
        out_specs=(P("section", "seq", None), P("section", "seq", None)),
        check_vma=False,
    )
```

```python
import functools
import math

import jax
import jax.numpy as jnp
from jax import lax
from jax.experimental import pallas as pl
from jax.experimental.pallas import tpu as pltpu
from jax.sharding import PartitionSpec as P

HEADS = 24
FEAT = 16
VDIM = 128
PACKED = 160
HALF = HEADS // 2
STEP_HEADS = 4
STEPS = HEADS // STEP_HEADS
STEP_LANES = STEP_HEADS * VDIM
HALF_STATE = HALF * PACKED
CHIPS = 16
PIECES = 4

EPSILON = 1e-06
SCORE_SCALE = 1.0 / math.sqrt(FEAT)
LINEAR_SCALE = FEAT ** (-0.25)
PAIR_SCALE = 1.0 / math.sqrt(2.0 * FEAT)

f32 = jnp.float32
bf16 = jnp.bfloat16


def dot(a, b, contract):
    return lax.dot_general(a, b, (contract, ((), ())), preferred_element_type=f32)


IN_HBM = pl.BlockSpec(memory_space=pltpu.HBM)


def params(micros, limit_mib=16):
    return dict(
        compiler_params=pltpu.CompilerParams(vmem_limit_bytes=limit_mib << 20),
        cost_estimate=pl.CostEstimate(flops=int(micros * 1.1e9), bytes_accessed=1 << 16, transcendentals=0),
    )


def shaped(*shapes):
    return [jax.ShapeDtypeStruct(dims, dtype) for dims, dtype in shapes]


def streamed(kernel, operands, out_shape, name, micros, scratch, copies, limit_mib=62):
    return pl.pallas_call(
        kernel,
        in_specs=[IN_HBM] * len(operands),
        out_specs=[IN_HBM] * len(out_shape),
        out_shape=shaped(*out_shape),
        scratch_shapes=[pltpu.VMEM(dims, dtype) for dims, dtype in scratch] + [pltpu.SemaphoreType.DMA((copies,))],
        name=name,
        **params(micros, limit_mib),
    )(*operands)


class Copies:
    def __init__(self, sems):
        self.sems, self.used = sems, 0

    def make(self, source, target):
        self.used += 1
        return pltpu.make_async_copy(source, target, self.last())

    def last(self):
        return self.sems.at[self.used - 1]

    def start(self, source, target):
        copy = self.make(source, target)
        copy.start()
        return copy


def wait_all(copies):
    for copy in copies:
        copy.wait()


def rolled(block, distance):
    return pltpu.roll(block, distance % block.shape[0], 0)


def taylor_rows(cols, pair_weight):
    pieces = []
    for distance in range(FEAT // 2 + 1):
        if distance == 0:
            product = cols * cols * PAIR_SCALE
        else:
            product = cols * rolled(cols, -distance) * (PAIR_SCALE * pair_weight)
        pieces.append(product if distance < FEAT // 2 else product[: FEAT // 2])
    row = lax.broadcasted_iota(jnp.int32, (FEAT // 2, cols.shape[1]), 0)
    pieces.append(jnp.where(row == 0, 1.0, 0.0).astype(f32))
    pieces.append(cols * LINEAR_SCALE)
    return jnp.concatenate(pieces, axis=0).astype(bf16)


def taylor_back(cols, grad_rows, pair_weight):
    mixed = 2.0 * grad_rows[:FEAT] * cols
    for distance in range(1, FEAT // 2):
        part = grad_rows[FEAT * distance : FEAT * (distance + 1)]
        term = part * rolled(cols, -distance) + rolled(part * cols, distance)
        mixed = mixed + (term if pair_weight == 1.0 else pair_weight * term)
    half = FEAT // 2
    last = grad_rows[FEAT * half : FEAT * half + half]
    term = jnp.concatenate([last * cols[half:], last * cols[:half]], axis=0)
    mixed = mixed + (term if pair_weight == 1.0 else pair_weight * term)
    return grad_rows[PACKED - FEAT :] * LINEAR_SCALE + mixed * PAIR_SCALE


def head_of(index, size):
    return slice(index * size, (index + 1) * size)


def core_here():
    return lax.rem(lax.axis_index("seq"), 2)


def lanes_of(step):
    return slice(step * STEP_LANES, (step + 1) * STEP_LANES)


def half_rows(half):
    return pl.ds(pl.multiple_of(half * HALF_STATE, HALF_STATE), HALF_STATE)


def by_lanes(copies, source, target, steps=range(STEPS)):
    return [copies.start(source.at[:, lanes_of(step)], target.at[:, lanes_of(step)]) for step in steps]


def state_out(copies, core, step, state_ref, own_hbm, away_hbm):
    rows = STEP_HEADS * PACKED
    source = state_ref.at[head_of(step, rows)]
    here = head_of(step % (STEPS // 2), rows)
    is_own = core == step // (STEPS // 2)
    to_own = copies.make(source, own_hbm.at[here])
    to_away = pltpu.make_async_copy(source, away_hbm.at[here], copies.last())
    pl.when(is_own)(to_own.start)
    pl.when(jnp.logical_not(is_own))(to_away.start)
    return to_own


def state_kernel(
    x_hbm,
    gain_hbm,
    query_hbm,
    key_hbm,
    before_hbm,
    taps_hbm,
    values_hbm,
    cols_hbm,
    own_hbm,
    away_hbm,
    x_ref,
    gain_ref,
    weight_ref,
    before_ref,
    taps_ref,
    normed_ref,
    values_ref,
    cols_ref,
    state_ref,
    sems,
):
    copies = Copies(sems)
    middle = query_hbm.shape[1]
    rows = x_ref.shape[0]
    first = [copies.start(x_hbm, x_ref), copies.start(gain_hbm, gain_ref)]
    small = [copies.start(before_hbm, before_ref), copies.start(taps_hbm, taps_ref)]
    weights = []
    for step in range(STEPS):
        here = lanes_of(step)
        to_query = copies.start(query_hbm.at[here], weight_ref.at[here, :middle])
        weights.append([to_query, copies.start(key_hbm.at[here], weight_ref.at[here, middle:])])
    wait_all(first)

    def normed_rows(x):
        x = x.astype(f32)
        inv_rms = lax.rsqrt(jnp.mean(x * x, axis=1, keepdims=True) + EPSILON)
        return (x * inv_rms * gain_ref[...]).astype(bf16)

    @pl.loop(0, rows // 16, unroll=4)
    def _(step):
        here = pl.ds(pl.multiple_of(step * 16, 16), 16)
        normed_ref[here] = normed_rows(x_ref[here])

    core = core_here()
    wait_all(small)
    edge = before_ref.shape[0]
    before_ref[...] = normed_rows(before_ref[...])
    out = []
    for step in range(STEPS):
        lanes = lanes_of(step)
        normed = normed_ref[:, lanes].astype(f32)
        before = before_ref[:, lanes].astype(f32)[edge - 8 :]
        row = lax.broadcasted_iota(jnp.int32, normed.shape, 0)
        one_back = jnp.where(row == 0, before[7:8], rolled(normed, 1))
        two_back = jnp.where(row == 0, before[6:7], rolled(one_back, 1))
        taps = [taps_ref[tap, :, lanes] for tap in range(3)]
        values = (taps[0] * two_back + taps[1] * one_back + taps[2] * normed).astype(bf16)
        values_ref[:, lanes] = values
        out += by_lanes(copies, values_ref, values_hbm, [step])
        wait_all(weights[step])
        product = dot(normed_ref[:, lanes], weight_ref[lanes], ((1,), (0,)))
        total = product if step == 0 else total + product
    cols_ref[...] = total.T.astype(bf16)
    out.append(copies.start(cols_ref, cols_hbm))
    for step in range(STEPS):
        for place in range(step * STEP_HEADS, (step + 1) * STEP_HEADS):
            keys = cols_ref[middle + place * FEAT : middle + (place + 1) * FEAT].astype(f32)
            state = dot(taylor_rows(keys, 1.0), values_ref[:, head_of(place, VDIM)], ((1,), (0,)))
            state_ref[head_of(place, PACKED)] = state.astype(bf16)
        out.append(state_out(copies, core, step, state_ref, own_hbm, away_hbm))
    wait_all(out)


def causal(rows):
    token = lax.broadcasted_iota(jnp.int32, (rows, rows), 0)
    other = lax.broadcasted_iota(jnp.int32, (rows, rows), 1)
    return token >= other, other >= token


def half_lanes(half):
    return slice(half * HALF * VDIM, (half + 1) * HALF * VDIM)


def inside_kernel(half, cols_hbm, values_hbm, inside_hbm, cols_ref, values_ref, inside_ref, sems):
    copies = Copies(sems)
    first = copies.start(cols_hbm, cols_ref)
    here = half_lanes(half)
    blocks = by_lanes(copies, values_hbm.at[:, here], values_ref, range(STEPS // 2))
    first.wait()
    middle, rows = cols_ref.shape[0] // 2, cols_ref.shape[1]
    mask, _ = causal(rows)
    out = []
    for step in range(STEPS // 2):
        blocks[step].wait()
        for head in range(STEP_HEADS):
            place = half * HALF + step * STEP_HEADS + head
            query = cols_ref[head_of(place, FEAT)]
            key = cols_ref[middle + place * FEAT : middle + (place + 1) * FEAT]
            scores = dot(query, key, ((0,), (0,))) * SCORE_SCALE
            weights = jnp.where(mask, 1.0 + scores + 0.5 * scores * scores, 0.0).astype(bf16)
            lanes = head_of(step * STEP_HEADS + head, VDIM)
            inside_ref[:, lanes] = dot(weights, values_ref[:, lanes], ((1,), (0,))).astype(bf16)
        out += by_lanes(copies, inside_ref, inside_hbm, [step])
    wait_all(out)


def states_in(copies, core, before_hbm, other_hbm, theirs_hbm, state_ref, other_ref):
    return [
        copies.start(before_hbm, state_ref.at[half_rows(core)]),
        copies.start(other_hbm, other_ref),
        copies.start(theirs_hbm, state_ref.at[half_rows(1 - core)]),
    ]


def state_of(place, adds_other, state_ref, other_ref):
    half, within = place // HALF, place % HALF
    state = state_ref[head_of(place, PACKED)]
    both = add_states(state, other_ref[head_of(within, PACKED)])
    return jnp.where(adds_other[half], both, state)


def head_means(terms, other_terms, ones):
    both = jnp.concatenate([terms.astype(bf16), other_terms.astype(bf16)], axis=1)
    return dot(both, ones, ((1,), (0,))) * (1.0 / VDIM)


def output_kernel(
    cols_hbm,
    inside_low_hbm,
    inside_high_hbm,
    before_hbm,
    other_hbm,
    theirs_hbm,
    x_hbm,
    grad_hbm,
    scale_hbm,
    out_hbm,
    numer_hbm,
    prefix_hbm,
    grad_own_hbm,
    grad_away_hbm,
    cols_ref,
    inside_ref,
    prefix_ref,
    other_ref,
    x_ref,
    grad_ref,
    scale_ref,
    out_ref,
    numer_ref,
    state_ref,
    sems,
):
    copies = Copies(sems)
    core = core_here()
    middle = cols_ref.shape[0] // 2
    first = states_in(copies, core, before_hbm, other_hbm, theirs_hbm, prefix_ref, other_ref)
    first += [copies.start(cols_hbm.at[:middle], cols_ref.at[:middle]), copies.start(scale_hbm, scale_ref)]
    blocks = []
    for step in range(STEPS):
        source = inside_low_hbm if step < STEPS // 2 else inside_high_hbm
        blocks.append(
            [copies.start(source.at[:, lanes_of(step % (STEPS // 2))], inside_ref.at[:, lanes_of(step)])]
            + by_lanes(copies, x_hbm, x_ref, [step])
            + by_lanes(copies, grad_hbm, grad_ref, [step])
        )
    wait_all(first)
    adds_other = (False, core == 1)
    side = lax.broadcasted_iota(jnp.int32, (2 * VDIM, 2 * VDIM), 0) < VDIM
    other_side = lax.broadcasted_iota(jnp.int32, (2 * VDIM, 2 * VDIM), 1) < VDIM
    ones = jnp.where(side == other_side, 1.0, 0.0).astype(bf16)
    out = []
    for step in range(STEPS):
        wait_all(blocks[step])
        for head in range(STEP_HEADS):
            place = step * STEP_HEADS + head
            lanes = head_of(place, VDIM)
            feat = taylor_rows(cols_ref[head_of(place, FEAT)].astype(f32), 2.0)
            prefix = state_of(place, adds_other, prefix_ref, other_ref)
            prefix_ref[head_of(place, PACKED)] = prefix
            numer = inside_ref[:, lanes].astype(f32) + dot(feat, prefix, ((0,), (0,)))
            scale = scale_ref[:, lanes]
            grad = grad_ref[:, lanes].astype(f32) * scale
            means = head_means(numer * numer, grad * numer, ones)
            inv = lax.rsqrt(means[:, :VDIM] + EPSILON)
            mean = means[:, VDIM:]
            out_ref[:, lanes] = (x_ref[:, lanes].astype(f32) + scale * (numer * inv)).astype(bf16)
            grad_numer = (inv * grad - numer * (inv * inv * inv * mean)).astype(bf16)
            numer_ref[:, lanes] = grad_numer
            state_ref[head_of(place, PACKED)] = dot(feat, grad_numer, ((1,), (0,))).astype(bf16)
        state_rows = head_of(step, STEP_HEADS * PACKED)
        out.append(state_out(copies, core, step, state_ref, grad_own_hbm, grad_away_hbm))
        out += by_lanes(copies, out_ref, out_hbm, [step]) + by_lanes(copies, numer_ref, numer_hbm, [step])
        out.append(copies.start(prefix_ref.at[state_rows], prefix_hbm.at[state_rows]))
    wait_all(out)


def inside_back_kernel(
    half,
    cols_hbm,
    values_hbm,
    numer_hbm,
    prefix_hbm,
    grad_cols_hbm,
    grad_values_hbm,
    cols_ref,
    values_ref,
    numer_ref,
    prefix_ref,
    grad_cols_ref,
    grad_values_ref,
    sems,
):
    copies = Copies(sems)
    here = half_lanes(half)
    steps = range(STEPS // 2)
    first = [copies.start(cols_hbm, cols_ref)]
    state_rows = slice(half * HALF_STATE, (half + 1) * HALF_STATE)
    blocks = [
        by_lanes(copies, numer_hbm.at[:, here], numer_ref, [step])
        + by_lanes(copies, values_hbm.at[:, here], values_ref, [step])
        for step in steps
    ]
    first.append(copies.start(prefix_hbm.at[state_rows], prefix_ref))
    wait_all(first)
    middle, rows = cols_ref.shape[0] // 2, cols_ref.shape[1]
    mask, turned_mask = causal(rows)
    out = []
    for step in steps:
        wait_all(blocks[step])
        for head in range(STEP_HEADS):
            within = step * STEP_HEADS + head
            place = half * HALF + within
            lanes = head_of(within, VDIM)
            query = cols_ref[head_of(place, FEAT)]
            key = cols_ref[middle + place * FEAT : middle + (place + 1) * FEAT]
            grad_numer, values = numer_ref[:, lanes], values_ref[:, lanes]
            scores = dot(query, key, ((0,), (0,))) * SCORE_SCALE
            turned = dot(key, query, ((0,), (0,))) * SCORE_SCALE
            weights = jnp.where(turned_mask, 1.0 + turned + 0.5 * turned * turned, 0.0).astype(bf16)
            grad_values_ref[:, lanes] = dot(weights, grad_numer, ((1,), (0,))).astype(bf16)
            grad_weights = dot(grad_numer, values, ((1,), (1,)))
            grad_scores = jnp.where(mask, grad_weights * (1.0 + scores), 0.0).astype(bf16)
            grad_query = dot(key, grad_scores, ((1,), (1,))) * SCORE_SCALE
            grad_key = dot(query, grad_scores, ((1,), (0,))) * SCORE_SCALE
            grad_feat = dot(prefix_ref[head_of(within, PACKED)], grad_numer, ((1,), (1,)))
            grad_cols_ref[head_of(within, FEAT)] = grad_query + taylor_back(query.astype(f32), grad_feat, 2.0)
            grad_cols_ref[head_of(HALF + within, FEAT)] = grad_key
        out += by_lanes(copies, grad_values_ref, grad_values_hbm, [step])
    out.append(copies.start(grad_cols_ref, grad_cols_hbm))
    wait_all(out)


def late_kernel(
    cols_hbm,
    values_hbm,
    before_hbm,
    other_hbm,
    theirs_hbm,
    cols_low_hbm,
    cols_high_hbm,
    values_low_hbm,
    values_high_hbm,
    query_hbm,
    key_hbm,
    taps_hbm,
    gain_hbm,
    x_hbm,
    grad_hbm,
    *rest,
):
    edge_hbm, scaled_hbm, sums_hbm = rest[:3]
    piece_hbms, rest = rest[3 : 2 + PIECES], rest[2 + PIECES :]
    (
        cols_ref,
        values_ref,
        state_ref,
        other_ref,
        grads_ref,
        early_ref,
        weight_ref,
        taps_ref,
        gain_ref,
        x_ref,
        grad_ref,
        grad_values_ref,
        turned_ref,
        scaled_ref,
        sums_ref,
        out_ref,
        edge_ref,
        sems,
    ) = rest
    copies = Copies(sems)
    core = core_here()
    middle, rows = cols_ref.shape[0], cols_ref.shape[1]
    half_cols = middle // 2
    first = states_in(copies, core, before_hbm, other_hbm, theirs_hbm, state_ref, other_ref)
    first.append(copies.start(cols_hbm.at[middle:], cols_ref))
    for half, source in enumerate((cols_low_hbm, cols_high_hbm)):
        for kind in range(2):
            start = kind * middle + half * half_cols
            first.append(
                copies.start(
                    source.at[kind * half_cols : (kind + 1) * half_cols], grads_ref.at[start : start + half_cols]
                )
            )
    blocks = []
    for step in range(STEPS):
        source = values_low_hbm if step < STEPS // 2 else values_high_hbm
        blocks.append(
            by_lanes(copies, values_hbm, values_ref, [step])
            + [copies.start(source.at[:, lanes_of(step % (STEPS // 2))], early_ref.at[:, lanes_of(step)])]
        )
    first += [copies.start(taps_hbm, taps_ref), copies.start(gain_hbm, gain_ref)]
    weights = []
    for step in range(STEPS):
        lanes = lanes_of(step)
        weights.append(copies.start(query_hbm.at[lanes], weight_ref.at[lanes, :middle]))
        weights.append(copies.start(key_hbm.at[lanes], weight_ref.at[lanes, middle:]))
    weights.append(copies.start(x_hbm, x_ref))
    grad_in = copies.start(grad_hbm, grad_ref)
    wait_all(first)
    adds_other = (core == 0, False)
    for step in range(STEPS):
        wait_all(blocks[step])
        for head in range(STEP_HEADS):
            place = step * STEP_HEADS + head
            lanes = head_of(place, VDIM)
            key = cols_ref[head_of(place, FEAT)].astype(f32)
            state = state_of(place, adds_other, state_ref, other_ref)
            grad_feat = dot(state, values_ref[:, lanes], ((1,), (1,)))
            key_rows = slice(middle + place * FEAT, middle + (place + 1) * FEAT)
            grads_ref[key_rows] = grads_ref[key_rows] + taylor_back(key, grad_feat, 1.0)
            late = dot(taylor_rows(key, 1.0), state, ((0,), (0,)))
            grad_values_ref[:, lanes] = early_ref[:, lanes].astype(f32) + late
    edge_ref[...] = grad_values_ref[:8]
    out = [copies.start(edge_ref, edge_hbm)]
    turned_ref[...] = grads_ref[...].T.astype(bf16)
    wait_all(weights)
    total = jnp.zeros((rows, VDIM), f32)
    squares = jnp.zeros((rows, VDIM), f32)
    for step in range(STEPS):
        lanes = lanes_of(step)
        grad_values = grad_values_ref[:, lanes]
        row = lax.broadcasted_iota(jnp.int32, grad_values.shape, 0)
        one_on = jnp.where(row == rows - 1, 0.0, rolled(grad_values, -1))
        two_on = jnp.where(row == rows - 1, 0.0, rolled(one_on, -1))
        grad_normed = dot(turned_ref[...], weight_ref[lanes], ((1,), (1,)))
        taps = [taps_ref[tap, :, lanes] for tap in range(3)]
        grad_normed = grad_normed + (taps[2] * grad_values + taps[1] * one_on + taps[0] * two_on)
        scaled = grad_normed * gain_ref[:, lanes]
        scaled_ref[:, lanes] = scaled
        x = x_ref[:, lanes].astype(f32)
        for head in range(STEP_HEADS):
            x_part, scaled_part = x[:, head_of(head, VDIM)], scaled[:, head_of(head, VDIM)]
            total = total + x_part * scaled_part
            squares = squares + x_part * x_part
    total = jnp.sum(total, axis=1, keepdims=True)
    squares = jnp.sum(squares, axis=1, keepdims=True)
    lane = lax.broadcasted_iota(jnp.int32, (rows, VDIM), 1)
    sums_ref[...] = jnp.where(lane == 0, total, jnp.where(lane == 1, squares, 0.0))
    cut = rows // PIECES
    tail = slice(rows - cut, rows)
    out += [copies.start(scaled_ref.at[tail], scaled_hbm), copies.start(sums_ref.at[tail], sums_hbm)]
    grad_in.wait()
    for piece in range(PIECES - 1):
        here = slice(piece * cut, (piece + 1) * cut)
        out_ref[here] = input_grad(scaled_ref[here], sums_ref[here], x_ref[here], grad_ref[here])
        out.append(copies.start(out_ref.at[here], piece_hbms[piece]))
    wait_all(out)


def input_grad(scaled, sums, x, grad):
    width = x.shape[1]
    inv = lax.rsqrt(sums[:, 1:2] / width + EPSILON)
    pull = inv * inv * inv * (sums[:, 0:1] / width)
    return (grad.astype(f32) + inv * scaled - x.astype(f32) * pull).astype(bf16)


def last_kernel(*refs):
    scaled_hbm, sums_hbm, x_hbm, grad_hbm, after_hbm, taps_hbm, gain_hbm, forward_hbm, out_hbm, forward_out_hbm = refs[:10]
    scaled_ref, sums_ref, x_ref, grad_ref, after_ref, taps_ref, gain_ref, out_ref, forward_ref, sems = refs[10:]
    copies = Copies(sems)
    rows, width = x_ref.shape
    tail = slice(x_hbm.shape[0] - rows, x_hbm.shape[0])
    sources = [scaled_hbm, sums_hbm, x_hbm.at[tail], grad_hbm.at[tail], after_hbm, taps_hbm, gain_hbm]
    targets = [scaled_ref, sums_ref, x_ref, grad_ref, after_ref, taps_ref, gain_ref]
    first = [copies.start(source, target) for source, target in zip(sources, targets)]
    forward = copies.start(forward_hbm, forward_ref)
    wait_all(first)
    after = after_ref[...]
    row = lax.broadcasted_iota(jnp.int32, (rows, width), 0)
    upper = taps_ref[0] * after[0:1]
    lower = taps_ref[1] * after[0:1] + taps_ref[0] * after[1:2]
    extra = jnp.where(row == rows - 2, upper, jnp.where(row == rows - 1, lower, 0.0)) * gain_ref[...]
    with_x = jnp.sum(x_ref[...].astype(f32) * extra, axis=1, keepdims=True)
    lane = lax.broadcasted_iota(jnp.int32, sums_ref.shape, 1)
    sums = sums_ref[...] + jnp.where(lane == 0, with_x, 0.0)
    out_ref[...] = input_grad(scaled_ref[...] + extra, sums, x_ref[...], grad_ref[...])
    forward.wait()
    wait_all([copies.start(out_ref, out_hbm), copies.start(forward_ref, forward_out_hbm)])


def chip_sums_kernel(reverse, got_ref, out_ref):
    total = jnp.zeros(got_ref.shape[1:], f32)
    order = range(CHIPS - 1, -1, -1) if reverse else range(CHIPS)
    for chip in order:
        out_ref[chip] = total.astype(bf16)
        total = total + got_ref[chip].astype(f32)


def chip_sums(got, reverse):
    return pl.pallas_call(
        functools.partial(chip_sums_kernel, reverse),
        out_shape=jax.ShapeDtypeStruct(got.shape, bf16),
        name="chip_sums",
        **params(0.8),
    )(got)


def pair_sum_kernel(own_ref, other_ref, out_ref):
    rows = out_ref.shape[1]
    for chip in range(CHIPS):
        here = head_of(chip, rows)
        out_ref[chip] = add_states(own_ref[here], other_ref[here])


def pair_sum(own, other):
    return pl.pallas_call(
        pair_sum_kernel,
        out_shape=jax.ShapeDtypeStruct((CHIPS, own.shape[0] // CHIPS, VDIM), bf16),
        name="pair_sum",
        **params(0.5),
    )(own, other)


def core_swap(block):
    count = lax.axis_size("seq")
    return lax.ppermute(block, "seq", [(i, i ^ 1) for i in range(count)])


def over_chips(block):
    count = lax.axis_size("seq")
    groups = [list(range(core, count, 2)) for core in range(2)]
    return lax.all_to_all(block, "seq", 0, 0, tiled=True, axis_index_groups=groups)


def add_states(one, other):
    return (one.astype(f32) + other.astype(f32)).astype(bf16)


def scan_first(away, own):
    other = core_swap(away)
    return over_chips(pair_sum(own, other)), other


def scan_second(before, own, counts_own):
    before = before.reshape(own.shape)
    theirs = core_swap(jnp.where(counts_own, add_states(before, own), before))
    return before, theirs


def neighbour_rows(edge, distance):
    devices = range(lax.axis_size("seq"))
    route = [(i - distance, i) for i in devices if i - distance in devices]
    return lax.ppermute(edge, "seq", route)


def section_pass(block, distance):
    count = lax.axis_size("section")
    return lax.ppermute(block, "section", [((i - distance) % count, i) for i in range(count)])


def local(layer_in, norm_gain, conv_weight, query_weight, key_weight, out_gain, layer_grad):
    x, grad = layer_in[0], layer_grad[0]
    query_proj, key_proj = query_weight[0], key_weight[0]
    taps = jnp.transpose(conv_weight, (1, 0, 2))
    rows, width = x.shape
    both = 2 * query_proj.shape[1]
    half_width = width // 2
    cut = rows // PIECES
    parity = core_here()
    half_state = ((HALF_STATE, VDIM), bf16)
    all_state = ((2 * HALF_STATE, VDIM), bf16)
    tokens, tokens_wide = ((rows, width), bf16), ((rows, width), f32)
    cols_shape = ((both, rows), bf16)

    before_edge = neighbour_rows(x[rows - 16 :], 1)
    values, cols, own, away = streamed(
        state_kernel,
        [x, norm_gain, query_proj, key_proj, before_edge, taps],
        [tokens, cols_shape, half_state, half_state],
        "state",
        8,
        [tokens, ((1, width), f32), ((width, both), bf16), ((16, width), bf16), ((3, 1, width), f32)]
        + [tokens, tokens, cols_shape, all_state],
        4 + 2 * STEPS + 1 + 2 * STEPS,
    )

    def inside(half, cols, values):
        shape = ((rows, half_width), bf16)
        return streamed(
            functools.partial(inside_kernel, half),
            [cols, values],
            [shape],
            "inside",
            3,
            [cols_shape, shape, shape],
            1 + STEPS,
        )[0]

    got, other = scan_first(away, own)
    got, inside_low = lax.optimization_barrier((got, inside(0, cols, values)))
    _, values_then = lax.optimization_barrier((got, values))
    before, inside_high = lax.optimization_barrier((over_chips(chip_sums(got, False)), inside(1, cols, values_then)))
    before, theirs = scan_second(before, own, parity == 0)
    output, numer, prefix, grad_own, grad_away = streamed(
        output_kernel,
        [cols, inside_low, inside_high, before, other, theirs, x, grad, out_gain],
        [tokens, tokens, all_state, half_state, half_state],
        "output",
        8,
        [cols_shape, tokens, all_state, half_state, tokens, tokens, ((1, width), f32), tokens, tokens, all_state],
        5 + 3 * STEPS + 4 * STEPS,
    )
    sent_forward = section_pass(output, 1)

    def inside_back(half, numer):
        shape = ((rows, half_width), bf16)
        grads = ((both // 2, rows), f32)
        return streamed(
            functools.partial(inside_back_kernel, half),
            [cols, values, numer, prefix],
            [grads, shape],
            "inside_back",
            5,
            [cols_shape, shape, shape, half_state, grads, shape],
            2 + 3 * (STEPS // 2) + 1,
        )

    got, grad_other = scan_first(grad_away, grad_own)
    got, low = lax.optimization_barrier((got, inside_back(0, numer)))
    _, numer_then = lax.optimization_barrier((got, numer))
    grad_before, high = lax.optimization_barrier((over_chips(chip_sums(got, True)), inside_back(1, numer_then)))
    grad_before, grad_theirs = scan_second(grad_before, grad_own, parity == 1)
    edge, scaled, sums, *pieces = streamed(
        late_kernel,
        [cols, values, grad_before, grad_other, grad_theirs, low[0], high[0], low[1], high[1]]
        + [query_proj, key_proj, taps, norm_gain, x, grad],
        [((8, width), f32), ((cut, width), f32), ((cut, VDIM), f32)] + [((cut, width), bf16)] * (PIECES - 1),
        "late",
        9,
        [((both // 2, rows), bf16), tokens, all_state, half_state, ((both, rows), f32), tokens]
        + [((width, both), bf16)]
        + [((3, 1, width), f32), ((1, width), f32), tokens, tokens, tokens_wide, ((rows, both), bf16), tokens_wide]
        + [((rows, VDIM), f32), tokens, ((8, width), f32)],
        3 + 1 + 4 + 2 * STEPS + 2 + 2 * STEPS + 2 + 1 + 2 + PIECES - 1,
    )
    after_edge = neighbour_rows(edge, -1)
    piece_wide, piece = ((cut, width), f32), ((cut, width), bf16)
    last_piece, sent_forward = streamed(
        last_kernel,
        [scaled, sums, x, grad, after_edge, taps, norm_gain, sent_forward],
        [piece, tokens],
        "last",
        2,
        [piece_wide, ((cut, VDIM), f32), piece, piece, ((8, width), f32), ((3, 1, width), f32), ((1, width), f32)]
        + [piece, tokens],
        10,
    )
    pieces.append(last_piece)
    sent_backward = jnp.concatenate([section_pass(piece, -1) for piece in pieces], axis=0)
    return (sent_forward[None], sent_backward[None])


def solution(mesh):
    return jax.shard_map(
        local,
        mesh=mesh,
        in_specs=(
            P("section", "seq", None),
            P("section", None),
            P("section", None, None),
            P("section", None, None),
            P("section", None, None),
            P("section", None),
            P("section", "seq", None),
        ),
        out_specs=(P("section", "seq", None), P("section", "seq", None)),
        check_vma=False,
    )
```

```python
import functools
import math

import jax
import jax.numpy as jnp
from jax import lax
from jax.experimental import pallas as pl
from jax.experimental.pallas import tpu as pltpu
from jax.sharding import PartitionSpec as P

HEADS = 24
FEAT = 16
VDIM = 128
PACKED = 160
HALF = HEADS // 2
STEP_HEADS = 4
STEPS = HEADS // STEP_HEADS
STEP_LANES = STEP_HEADS * VDIM
HALF_STATE = HALF * PACKED
CHIPS = 16
PIECES = 4

EPSILON = 1e-06
SCORE_SCALE = 1.0 / math.sqrt(FEAT)
LINEAR_SCALE = FEAT ** (-0.25)
PAIR_SCALE = 1.0 / math.sqrt(2.0 * FEAT)

f32 = jnp.float32
bf16 = jnp.bfloat16


def dot(a, b, contract):
    return lax.dot_general(a, b, (contract, ((), ())), preferred_element_type=f32)


IN_HBM = pl.BlockSpec(memory_space=pltpu.HBM)


def params(micros, limit_mib=16):
    return dict(
        compiler_params=pltpu.CompilerParams(vmem_limit_bytes=limit_mib << 20),
        cost_estimate=pl.CostEstimate(flops=int(micros * 1.1e9), bytes_accessed=1 << 16, transcendentals=0),
    )


def shaped(*shapes):
    return [jax.ShapeDtypeStruct(dims, dtype) for dims, dtype in shapes]


def streamed(kernel, operands, out_shape, name, micros, scratch, copies, aliases=None, limit_mib=62):
    return pl.pallas_call(
        kernel,
        in_specs=[IN_HBM] * len(operands),
        out_specs=[IN_HBM] * len(out_shape),
        out_shape=shaped(*out_shape),
        scratch_shapes=[pltpu.VMEM(dims, dtype) for dims, dtype in scratch] + [pltpu.SemaphoreType.DMA((copies,))],
        input_output_aliases=aliases or {},
        name=name,
        **params(micros, limit_mib),
    )(*operands)


class Copies:
    def __init__(self, sems):
        self.sems, self.used = sems, 0

    def make(self, source, target):
        self.used += 1
        return pltpu.make_async_copy(source, target, self.last())

    def last(self):
        return self.sems.at[self.used - 1]

    def start(self, source, target):
        copy = self.make(source, target)
        copy.start()
        return copy


def wait_all(copies):
    for copy in copies:
        copy.wait()


def rolled(block, distance):
    return pltpu.roll(block, distance % block.shape[0], 0)


def taylor_rows(cols, pair_weight):
    pieces = []
    for distance in range(FEAT // 2 + 1):
        if distance == 0:
            product = cols * cols * PAIR_SCALE
        else:
            product = cols * rolled(cols, -distance) * (PAIR_SCALE * pair_weight)
        pieces.append(product if distance < FEAT // 2 else product[: FEAT // 2])
    row = lax.broadcasted_iota(jnp.int32, (FEAT // 2, cols.shape[1]), 0)
    pieces.append(jnp.where(row == 0, 1.0, 0.0).astype(f32))
    pieces.append(cols * LINEAR_SCALE)
    return jnp.concatenate(pieces, axis=0).astype(bf16)


def taylor_back(cols, grad_rows, pair_weight):
    mixed = 2.0 * grad_rows[:FEAT] * cols
    for distance in range(1, FEAT // 2):
        part = grad_rows[FEAT * distance : FEAT * (distance + 1)]
        term = part * rolled(cols, -distance) + rolled(part * cols, distance)
        mixed = mixed + (term if pair_weight == 1.0 else pair_weight * term)
    half = FEAT // 2
    last = grad_rows[FEAT * half : FEAT * half + half]
    term = jnp.concatenate([last * cols[half:], last * cols[:half]], axis=0)
    mixed = mixed + (term if pair_weight == 1.0 else pair_weight * term)
    return grad_rows[PACKED - FEAT :] * LINEAR_SCALE + mixed * PAIR_SCALE


def head_of(index, size):
    return slice(index * size, (index + 1) * size)


def core_here():
    return lax.rem(lax.axis_index("seq"), 2)


def lanes_of(step):
    return slice(step * STEP_LANES, (step + 1) * STEP_LANES)


def half_rows(half):
    return pl.ds(pl.multiple_of(half * HALF_STATE, HALF_STATE), HALF_STATE)


def by_lanes(copies, source, target, steps=range(STEPS)):
    return [copies.start(source.at[:, lanes_of(step)], target.at[:, lanes_of(step)]) for step in steps]


def state_out(copies, core, step, state_ref, own_hbm, away_hbm):
    rows = STEP_HEADS * PACKED
    source = state_ref.at[head_of(step, rows)]
    here = head_of(step % (STEPS // 2), rows)
    is_own = core == step // (STEPS // 2)
    to_own = copies.make(source, own_hbm.at[here])
    to_away = pltpu.make_async_copy(source, away_hbm.at[here], copies.last())
    pl.when(is_own)(to_own.start)
    pl.when(jnp.logical_not(is_own))(to_away.start)
    return to_own


def state_kernel(
    x_hbm,
    gain_hbm,
    query_hbm,
    key_hbm,
    before_hbm,
    taps_hbm,
    values_hbm,
    cols_hbm,
    own_hbm,
    away_hbm,
    x_ref,
    gain_ref,
    weight_ref,
    before_ref,
    taps_ref,
    normed_ref,
    values_ref,
    cols_ref,
    state_ref,
    sems,
):
    copies = Copies(sems)
    middle = query_hbm.shape[1]
    rows = x_ref.shape[0]
    first = [copies.start(x_hbm, x_ref), copies.start(gain_hbm, gain_ref)]
    small = [copies.start(before_hbm, before_ref), copies.start(taps_hbm, taps_ref)]
    weights = []
    for step in range(STEPS):
        here = lanes_of(step)
        to_query = copies.start(query_hbm.at[here], weight_ref.at[here, :middle])
        weights.append([to_query, copies.start(key_hbm.at[here], weight_ref.at[here, middle:])])
    wait_all(first)

    def normed_rows(x):
        x = x.astype(f32)
        inv_rms = lax.rsqrt(jnp.mean(x * x, axis=1, keepdims=True) + EPSILON)
        return (x * inv_rms * gain_ref[...]).astype(bf16)

    @pl.loop(0, rows // 16, unroll=4)
    def _(step):
        here = pl.ds(pl.multiple_of(step * 16, 16), 16)
        normed_ref[here] = normed_rows(x_ref[here])

    core = core_here()
    wait_all(small)
    edge = before_ref.shape[0]
    before_ref[...] = normed_rows(before_ref[...])
    out = []
    for step in range(STEPS):
        lanes = lanes_of(step)
        normed = normed_ref[:, lanes].astype(f32)
        before = before_ref[:, lanes].astype(f32)[edge - 8 :]
        row = lax.broadcasted_iota(jnp.int32, normed.shape, 0)
        one_back = jnp.where(row == 0, before[7:8], rolled(normed, 1))
        two_back = jnp.where(row == 0, before[6:7], rolled(one_back, 1))
        taps = [taps_ref[tap, :, lanes] for tap in range(3)]
        values = (taps[0] * two_back + taps[1] * one_back + taps[2] * normed).astype(bf16)
        values_ref[:, lanes] = values
        out += by_lanes(copies, values_ref, values_hbm, [step])
        wait_all(weights[step])
        product = dot(normed_ref[:, lanes], weight_ref[lanes], ((1,), (0,)))
        total = product if step == 0 else total + product
    cols_ref[...] = total.T.astype(bf16)
    out.append(copies.start(cols_ref, cols_hbm))
    for step in range(STEPS):
        for place in range(step * STEP_HEADS, (step + 1) * STEP_HEADS):
            keys = cols_ref[middle + place * FEAT : middle + (place + 1) * FEAT].astype(f32)
            state = dot(taylor_rows(keys, 1.0), values_ref[:, head_of(place, VDIM)], ((1,), (0,)))
            state_ref[head_of(place, PACKED)] = state.astype(bf16)
        out.append(state_out(copies, core, step, state_ref, own_hbm, away_hbm))
    wait_all(out)


def causal(rows):
    token = lax.broadcasted_iota(jnp.int32, (rows, rows), 0)
    other = lax.broadcasted_iota(jnp.int32, (rows, rows), 1)
    return token >= other, other >= token


def half_lanes(half):
    return slice(half * HALF * VDIM, (half + 1) * HALF * VDIM)


def inside_kernel(half, cols_hbm, values_hbm, inside_hbm, cols_ref, values_ref, inside_ref, sems):
    copies = Copies(sems)
    first = copies.start(cols_hbm, cols_ref)
    here = half_lanes(half)
    blocks = by_lanes(copies, values_hbm.at[:, here], values_ref, range(STEPS // 2))
    first.wait()
    middle, rows = cols_ref.shape[0] // 2, cols_ref.shape[1]
    mask, _ = causal(rows)
    out = []
    for step in range(STEPS // 2):
        blocks[step].wait()
        for head in range(STEP_HEADS):
            place = half * HALF + step * STEP_HEADS + head
            query = cols_ref[head_of(place, FEAT)]
            key = cols_ref[middle + place * FEAT : middle + (place + 1) * FEAT]
            scores = dot(query, key, ((0,), (0,))) * SCORE_SCALE
            weights = jnp.where(mask, 1.0 + scores + 0.5 * scores * scores, 0.0).astype(bf16)
            lanes = head_of(step * STEP_HEADS + head, VDIM)
            inside_ref[:, lanes] = dot(weights, values_ref[:, lanes], ((1,), (0,))).astype(bf16)
        out += by_lanes(copies, inside_ref, inside_hbm, [step])
    wait_all(out)


def states_in(copies, own_half, before_hbm, other_hbm, theirs_hbm, state_ref, other_ref):
    return [
        copies.start(before_hbm, state_ref.at[half_rows(own_half)]),
        copies.start(other_hbm, other_ref),
        copies.start(theirs_hbm, state_ref.at[half_rows(1 - own_half)]),
    ]


def state_of(place, adds_other, state_ref, other_ref):
    half, within = place // HALF, place % HALF
    state = state_ref[head_of(place, PACKED)]
    both = add_states(state, other_ref[head_of(within, PACKED)])
    return jnp.where(adds_other[half], both, state)


def head_means(terms, other_terms, ones):
    both = jnp.concatenate([terms.astype(bf16), other_terms.astype(bf16)], axis=1)
    return dot(both, ones, ((1,), (0,))) * (1.0 / VDIM)


def output_kernel(turn, cols_hbm, inside_low_hbm, inside_high_hbm, *refs):
    count = 2 if turn == 0 else 1
    state_hbms, refs = refs[:count], refs[count:]
    x_hbm, grad_hbm, scale_hbm = refs[:3]
    refs = refs[3 + 3 * turn :]
    out_hbm, numer_hbm, prefix_hbm, grads_hbm = refs[:4]
    cols_ref, inside_ref, prefix_ref, other_ref, x_ref, grad_ref, scale_ref, out_ref, numer_ref, state_ref, sems = refs[4:]
    copies = Copies(sems)
    core = core_here()
    half = core if turn == 0 else 1 - core
    half_lane, half_cols = HALF * VDIM, HALF * FEAT

    def at(step):
        return pl.ds(pl.multiple_of(half * half_lane + step * STEP_LANES, STEP_LANES), STEP_LANES)

    def rows_at(step):
        size = STEP_HEADS * PACKED
        return pl.ds(pl.multiple_of(half * HALF_STATE + step * size, size), size)

    first = [copies.start(state_hbms[0], prefix_ref)]
    if turn == 0:
        first.append(copies.start(state_hbms[1], other_ref))
    first.append(copies.start(cols_hbm.at[pl.ds(pl.multiple_of(half * half_cols, half_cols), half_cols)], cols_ref))
    first.append(copies.start(scale_hbm.at[:, pl.ds(pl.multiple_of(half * half_lane, half_lane), half_lane)], scale_ref))
    blocks = []
    for step in range(STEPS // 2):
        lanes = lanes_of(step)
        low = copies.make(inside_low_hbm.at[:, lanes], inside_ref.at[:, lanes])
        high = pltpu.make_async_copy(inside_high_hbm.at[:, lanes], inside_ref.at[:, lanes], copies.last())
        pl.when(half == 0)(low.start)
        pl.when(half != 0)(high.start)
        x_in = copies.start(x_hbm.at[:, at(step)], x_ref.at[:, lanes])
        blocks.append([low, x_in, copies.start(grad_hbm.at[:, at(step)], grad_ref.at[:, lanes])])
    wait_all(first)
    side = lax.broadcasted_iota(jnp.int32, (2 * VDIM, 2 * VDIM), 0) < VDIM
    other_side = lax.broadcasted_iota(jnp.int32, (2 * VDIM, 2 * VDIM), 1) < VDIM
    ones = jnp.where(side == other_side, 1.0, 0.0).astype(bf16)
    out = []
    for step in range(STEPS // 2):
        wait_all(blocks[step])
        for place in range(step * STEP_HEADS, (step + 1) * STEP_HEADS):
            lanes, state_rows = head_of(place, VDIM), head_of(place, PACKED)
            feat = taylor_rows(cols_ref[head_of(place, FEAT)].astype(f32), 2.0)
            prefix = prefix_ref[state_rows]
            if turn == 0:
                prefix = jnp.where(core == 1, add_states(prefix, other_ref[state_rows]), prefix)
                prefix_ref[state_rows] = prefix
            numer = inside_ref[:, lanes].astype(f32) + dot(feat, prefix, ((0,), (0,)))
            scale = scale_ref[:, lanes]
            grad = grad_ref[:, lanes].astype(f32) * scale
            means = head_means(numer * numer, grad * numer, ones)
            inv = lax.rsqrt(means[:, :VDIM] + EPSILON)
            mean = means[:, VDIM:]
            out_ref[:, lanes] = (x_ref[:, lanes].astype(f32) + scale * (numer * inv)).astype(bf16)
            grad_numer = (inv * grad - numer * (inv * inv * inv * mean)).astype(bf16)
            numer_ref[:, lanes] = grad_numer
            state_ref[state_rows] = dot(feat, grad_numer, ((1,), (0,))).astype(bf16)
        state_rows, lanes = head_of(step, STEP_HEADS * PACKED), lanes_of(step)
        out.append(copies.start(state_ref.at[state_rows], grads_hbm.at[state_rows]))
        out.append(copies.start(out_ref.at[:, lanes], out_hbm.at[:, at(step)]))
        out.append(copies.start(numer_ref.at[:, lanes], numer_hbm.at[:, at(step)]))
        out.append(copies.start(prefix_ref.at[state_rows], prefix_hbm.at[rows_at(step)]))
    wait_all(out)


def inside_back_kernel(
    half,
    cols_hbm,
    values_hbm,
    numer_hbm,
    prefix_hbm,
    grad_cols_hbm,
    grad_values_hbm,
    cols_ref,
    values_ref,
    numer_ref,
    prefix_ref,
    grad_cols_ref,
    grad_values_ref,
    sems,
):
    copies = Copies(sems)
    here = half_lanes(half)
    steps = range(STEPS // 2)
    first = [copies.start(cols_hbm, cols_ref)]
    state_rows = slice(half * HALF_STATE, (half + 1) * HALF_STATE)
    blocks = [
        by_lanes(copies, numer_hbm.at[:, here], numer_ref, [step])
        + by_lanes(copies, values_hbm.at[:, here], values_ref, [step])
        for step in steps
    ]
    first.append(copies.start(prefix_hbm.at[state_rows], prefix_ref))
    wait_all(first)
    middle, rows = cols_ref.shape[0] // 2, cols_ref.shape[1]
    mask, turned_mask = causal(rows)
    out = []
    for step in steps:
        wait_all(blocks[step])
        for head in range(STEP_HEADS):
            within = step * STEP_HEADS + head
            place = half * HALF + within
            lanes = head_of(within, VDIM)
            query = cols_ref[head_of(place, FEAT)]
            key = cols_ref[middle + place * FEAT : middle + (place + 1) * FEAT]
            grad_numer, values = numer_ref[:, lanes], values_ref[:, lanes]
            scores = dot(query, key, ((0,), (0,))) * SCORE_SCALE
            turned = dot(key, query, ((0,), (0,))) * SCORE_SCALE
            weights = jnp.where(turned_mask, 1.0 + turned + 0.5 * turned * turned, 0.0).astype(bf16)
            grad_values_ref[:, lanes] = dot(weights, grad_numer, ((1,), (0,))).astype(bf16)
            grad_weights = dot(grad_numer, values, ((1,), (1,)))
            grad_scores = jnp.where(mask, grad_weights * (1.0 + scores), 0.0).astype(bf16)
            grad_query = dot(key, grad_scores, ((1,), (1,))) * SCORE_SCALE
            grad_key = dot(query, grad_scores, ((1,), (0,))) * SCORE_SCALE
            grad_feat = dot(prefix_ref[head_of(within, PACKED)], grad_numer, ((1,), (1,)))
            grad_cols_ref[head_of(within, FEAT)] = grad_query + taylor_back(query.astype(f32), grad_feat, 2.0)
            grad_cols_ref[head_of(HALF + within, FEAT)] = grad_key
        out += by_lanes(copies, grad_values_ref, grad_values_hbm, [step])
    out.append(copies.start(grad_cols_ref, grad_cols_hbm))
    wait_all(out)


def late_kernel(
    cols_hbm,
    values_hbm,
    before_hbm,
    other_hbm,
    theirs_hbm,
    cols_low_hbm,
    cols_high_hbm,
    values_low_hbm,
    values_high_hbm,
    query_hbm,
    key_hbm,
    taps_hbm,
    gain_hbm,
    x_hbm,
    grad_hbm,
    *rest,
):
    edge_hbm, scaled_hbm, sums_hbm = rest[:3]
    piece_hbms, rest = rest[3 : 2 + PIECES], rest[2 + PIECES :]
    (
        cols_ref,
        values_ref,
        state_ref,
        other_ref,
        grads_ref,
        early_ref,
        weight_ref,
        taps_ref,
        gain_ref,
        x_ref,
        grad_ref,
        grad_values_ref,
        turned_ref,
        scaled_ref,
        sums_ref,
        out_ref,
        edge_ref,
        sems,
    ) = rest
    copies = Copies(sems)
    core = core_here()
    middle, rows = cols_ref.shape[0], cols_ref.shape[1]
    half_cols = middle // 2
    first = states_in(copies, 1 - core, before_hbm, other_hbm, theirs_hbm, state_ref, other_ref)
    first.append(copies.start(cols_hbm.at[middle:], cols_ref))
    for half, source in enumerate((cols_low_hbm, cols_high_hbm)):
        for kind in range(2):
            start = kind * middle + half * half_cols
            first.append(
                copies.start(
                    source.at[kind * half_cols : (kind + 1) * half_cols], grads_ref.at[start : start + half_cols]
                )
            )
    blocks = []
    for step in range(STEPS):
        source = values_low_hbm if step < STEPS // 2 else values_high_hbm
        blocks.append(
            by_lanes(copies, values_hbm, values_ref, [step])
            + [copies.start(source.at[:, lanes_of(step % (STEPS // 2))], early_ref.at[:, lanes_of(step)])]
        )
    first += [copies.start(taps_hbm, taps_ref), copies.start(gain_hbm, gain_ref)]
    weights = []
    for step in range(STEPS):
        lanes = lanes_of(step)
        weights.append(copies.start(query_hbm.at[lanes], weight_ref.at[lanes, :middle]))
        weights.append(copies.start(key_hbm.at[lanes], weight_ref.at[lanes, middle:]))
    weights.append(copies.start(x_hbm, x_ref))
    grad_in = copies.start(grad_hbm, grad_ref)
    wait_all(first)
    adds_other = (False, core == 0)
    for step in range(STEPS):
        wait_all(blocks[step])
        for head in range(STEP_HEADS):
            place = step * STEP_HEADS + head
            lanes = head_of(place, VDIM)
            key = cols_ref[head_of(place, FEAT)].astype(f32)
            state = state_of(place, adds_other, state_ref, other_ref)
            grad_feat = dot(state, values_ref[:, lanes], ((1,), (1,)))
            key_rows = slice(middle + place * FEAT, middle + (place + 1) * FEAT)
            grads_ref[key_rows] = grads_ref[key_rows] + taylor_back(key, grad_feat, 1.0)
            late = dot(taylor_rows(key, 1.0), state, ((0,), (0,)))
            grad_values_ref[:, lanes] = early_ref[:, lanes].astype(f32) + late
    edge_ref[...] = grad_values_ref[:8]
    out = [copies.start(edge_ref, edge_hbm)]
    turned_ref[...] = grads_ref[...].T.astype(bf16)
    wait_all(weights)
    total = jnp.zeros((rows, VDIM), f32)
    squares = jnp.zeros((rows, VDIM), f32)
    for step in range(STEPS):
        lanes = lanes_of(step)
        grad_values = grad_values_ref[:, lanes]
        row = lax.broadcasted_iota(jnp.int32, grad_values.shape, 0)
        one_on = jnp.where(row == rows - 1, 0.0, rolled(grad_values, -1))
        two_on = jnp.where(row == rows - 1, 0.0, rolled(one_on, -1))
        grad_normed = dot(turned_ref[...], weight_ref[lanes], ((1,), (1,)))
        taps = [taps_ref[tap, :, lanes] for tap in range(3)]
        grad_normed = grad_normed + (taps[2] * grad_values + taps[1] * one_on + taps[0] * two_on)
        scaled = grad_normed * gain_ref[:, lanes]
        scaled_ref[:, lanes] = scaled
        x = x_ref[:, lanes].astype(f32)
        for head in range(STEP_HEADS):
            x_part, scaled_part = x[:, head_of(head, VDIM)], scaled[:, head_of(head, VDIM)]
            total = total + x_part * scaled_part
            squares = squares + x_part * x_part
    total = jnp.sum(total, axis=1, keepdims=True)
    squares = jnp.sum(squares, axis=1, keepdims=True)
    lane = lax.broadcasted_iota(jnp.int32, (rows, VDIM), 1)
    sums_ref[...] = jnp.where(lane == 0, total, jnp.where(lane == 1, squares, 0.0))
    cut = rows // PIECES
    tail = slice(rows - cut, rows)
    out += [copies.start(scaled_ref.at[tail], scaled_hbm), copies.start(sums_ref.at[tail], sums_hbm)]
    grad_in.wait()
    for piece in range(PIECES - 1):
        here = slice(piece * cut, (piece + 1) * cut)
        out_ref[here] = input_grad(scaled_ref[here], sums_ref[here], x_ref[here], grad_ref[here])
        out.append(copies.start(out_ref.at[here], piece_hbms[piece]))
    wait_all(out)


def input_grad(scaled, sums, x, grad):
    width = x.shape[1]
    inv = lax.rsqrt(sums[:, 1:2] / width + EPSILON)
    pull = inv * inv * inv * (sums[:, 0:1] / width)
    return (grad.astype(f32) + inv * scaled - x.astype(f32) * pull).astype(bf16)


def last_kernel(*refs):
    scaled_hbm, sums_hbm, x_hbm, grad_hbm, after_hbm, taps_hbm, gain_hbm, forward_hbm, out_hbm, forward_out_hbm = refs[:10]
    scaled_ref, sums_ref, x_ref, grad_ref, after_ref, taps_ref, gain_ref, out_ref, forward_ref, sems = refs[10:]
    copies = Copies(sems)
    rows, width = x_ref.shape
    tail = slice(x_hbm.shape[0] - rows, x_hbm.shape[0])
    sources = [scaled_hbm, sums_hbm, x_hbm.at[tail], grad_hbm.at[tail], after_hbm, taps_hbm, gain_hbm]
    targets = [scaled_ref, sums_ref, x_ref, grad_ref, after_ref, taps_ref, gain_ref]
    first = [copies.start(source, target) for source, target in zip(sources, targets)]
    forward = copies.start(forward_hbm, forward_ref)
    wait_all(first)
    after = after_ref[...]
    row = lax.broadcasted_iota(jnp.int32, (rows, width), 0)
    upper = taps_ref[0] * after[0:1]
    lower = taps_ref[1] * after[0:1] + taps_ref[0] * after[1:2]
    extra = jnp.where(row == rows - 2, upper, jnp.where(row == rows - 1, lower, 0.0)) * gain_ref[...]
    with_x = jnp.sum(x_ref[...].astype(f32) * extra, axis=1, keepdims=True)
    lane = lax.broadcasted_iota(jnp.int32, sums_ref.shape, 1)
    sums = sums_ref[...] + jnp.where(lane == 0, with_x, 0.0)
    out_ref[...] = input_grad(scaled_ref[...] + extra, sums, x_ref[...], grad_ref[...])
    forward.wait()
    wait_all([copies.start(out_ref, out_hbm), copies.start(forward_ref, forward_out_hbm)])


def chip_sums_kernel(reverse, got_ref, out_ref):
    total = jnp.zeros(got_ref.shape[1:], f32)
    order = range(CHIPS - 1, -1, -1) if reverse else range(CHIPS)
    for chip in order:
        out_ref[chip] = total.astype(bf16)
        total = total + got_ref[chip].astype(f32)


def chip_sums(got, reverse):
    return pl.pallas_call(
        functools.partial(chip_sums_kernel, reverse),
        out_shape=jax.ShapeDtypeStruct(got.shape, bf16),
        name="chip_sums",
        **params(0.8),
    )(got)


def pair_sum_kernel(own_ref, other_ref, out_ref):
    rows = out_ref.shape[1]
    for chip in range(CHIPS):
        here = head_of(chip, rows)
        out_ref[chip] = add_states(own_ref[here], other_ref[here])


def pair_sum(own, other):
    return pl.pallas_call(
        pair_sum_kernel,
        out_shape=jax.ShapeDtypeStruct((CHIPS, own.shape[0] // CHIPS, VDIM), bf16),
        name="pair_sum",
        **params(0.5),
    )(own, other)


def core_swap(block):
    count = lax.axis_size("seq")
    return lax.ppermute(block, "seq", [(i, i ^ 1) for i in range(count)])


def over_chips(block):
    count = lax.axis_size("seq")
    groups = [list(range(core, count, 2)) for core in range(2)]
    return lax.all_to_all(block, "seq", 0, 0, tiled=True, axis_index_groups=groups)


def add_states(one, other):
    return (one.astype(f32) + other.astype(f32)).astype(bf16)


def scan_first(away, own):
    other = core_swap(away)
    return over_chips(pair_sum(own, other)), other


def scan_second(before, own, counts_own):
    before = before.reshape(own.shape)
    theirs = core_swap(jnp.where(counts_own, add_states(before, own), before))
    return before, theirs


def neighbour_rows(edge, distance):
    devices = range(lax.axis_size("seq"))
    route = [(i - distance, i) for i in devices if i - distance in devices]
    return lax.ppermute(edge, "seq", route)


def section_pass(block, distance):
    count = lax.axis_size("section")
    return lax.ppermute(block, "section", [((i - distance) % count, i) for i in range(count)])


def local(layer_in, norm_gain, conv_weight, query_weight, key_weight, out_gain, layer_grad):
    x, grad = layer_in[0], layer_grad[0]
    query_proj, key_proj = query_weight[0], key_weight[0]
    taps = jnp.transpose(conv_weight, (1, 0, 2))
    rows, width = x.shape
    both = 2 * query_proj.shape[1]
    half_width = width // 2
    cut = rows // PIECES
    parity = core_here()
    half_state = ((HALF_STATE, VDIM), bf16)
    all_state = ((2 * HALF_STATE, VDIM), bf16)
    tokens, tokens_wide = ((rows, width), bf16), ((rows, width), f32)
    cols_shape = ((both, rows), bf16)

    before_edge = neighbour_rows(x[rows - 16 :], 1)
    values, cols, own, away = streamed(
        state_kernel,
        [x, norm_gain, query_proj, key_proj, before_edge, taps],
        [tokens, cols_shape, half_state, half_state],
        "state",
        8,
        [tokens, ((1, width), f32), ((width, both), bf16), ((16, width), bf16), ((3, 1, width), f32)]
        + [tokens, tokens, cols_shape, all_state],
        4 + 2 * STEPS + 1 + 2 * STEPS,
    )

    def inside(half, cols, values):
        shape = ((rows, half_width), bf16)
        return streamed(
            functools.partial(inside_kernel, half),
            [cols, values],
            [shape],
            "inside",
            3,
            [cols_shape, shape, shape],
            1 + STEPS,
        )[0]

    got, other = scan_first(away, own)
    got, inside_low = lax.optimization_barrier((got, inside(0, cols, values)))
    _, values_then = lax.optimization_barrier((got, values))
    before, inside_high = lax.optimization_barrier((over_chips(chip_sums(got, False)), inside(1, cols, values_then)))
    before, theirs = scan_second(before, own, parity == 0)
    half_tokens = ((rows, half_width), bf16)

    def outputs(turn, states, filled):
        operands = [cols, inside_low, inside_high, *states, x, grad, out_gain, *filled]
        return streamed(
            functools.partial(output_kernel, turn),
            operands,
            [tokens, tokens, all_state, half_state],
            "output",
            5,
            [((both // 4, rows), bf16), half_tokens, half_state, half_state, half_tokens, half_tokens]
            + [((1, half_width), f32), half_tokens, half_tokens, half_state],
            4 + 3 * (STEPS // 2) + 4 * (STEPS // 2),
            aliases={len(operands) - len(filled) + k: k for k in range(len(filled))},
        )

    *filled, grad_away = outputs(0, [before, other], [])
    output, numer, prefix, grad_own = outputs(1, [theirs], filled)
    sent_forward = section_pass(output, 1)

    def inside_back(half, numer):
        shape = ((rows, half_width), bf16)
        grads = ((both // 2, rows), f32)
        return streamed(
            functools.partial(inside_back_kernel, half),
            [cols, values, numer, prefix],
            [grads, shape],
            "inside_back",
            5,
            [cols_shape, shape, shape, half_state, grads, shape],
            2 + 3 * (STEPS // 2) + 1,
        )

    got, grad_other = scan_first(grad_away, grad_own)
    got, low = lax.optimization_barrier((got, inside_back(0, numer)))
    _, numer_then = lax.optimization_barrier((got, numer))
    grad_before, high = lax.optimization_barrier((over_chips(chip_sums(got, True)), inside_back(1, numer_then)))
    grad_before, grad_theirs = scan_second(grad_before, grad_own, parity == 1)
    edge, scaled, sums, *pieces = streamed(
        late_kernel,
        [cols, values, grad_before, grad_other, grad_theirs, low[0], high[0], low[1], high[1]]
        + [query_proj, key_proj, taps, norm_gain, x, grad],
        [((8, width), f32), ((cut, width), f32), ((cut, VDIM), f32)] + [((cut, width), bf16)] * (PIECES - 1),
        "late",
        9,
        [((both // 2, rows), bf16), tokens, all_state, half_state, ((both, rows), f32), tokens]
        + [((width, both), bf16)]
        + [((3, 1, width), f32), ((1, width), f32), tokens, tokens, tokens_wide, ((rows, both), bf16), tokens_wide]
        + [((rows, VDIM), f32), tokens, ((8, width), f32)],
        3 + 1 + 4 + 2 * STEPS + 2 + 2 * STEPS + 2 + 1 + 2 + PIECES - 1,
    )
    after_edge = neighbour_rows(edge, -1)
    piece_wide, piece = ((cut, width), f32), ((cut, width), bf16)
    last_piece, sent_forward = streamed(
        last_kernel,
        [scaled, sums, x, grad, after_edge, taps, norm_gain, sent_forward],
        [piece, tokens],
        "last",
        2,
        [piece_wide, ((cut, VDIM), f32), piece, piece, ((8, width), f32), ((3, 1, width), f32), ((1, width), f32)]
        + [piece, tokens],
        10,
    )
    pieces.append(last_piece)
    sent_backward = jnp.concatenate([section_pass(piece, -1) for piece in pieces], axis=0)
    return (sent_forward[None], sent_backward[None])


def solution(mesh):
    return jax.shard_map(
        local,
        mesh=mesh,
        in_specs=(
            P("section", "seq", None),
            P("section", None),
            P("section", None, None),
            P("section", None, None),
            P("section", None, None),
            P("section", None),
            P("section", "seq", None),
        ),
        out_specs=(P("section", "seq", None), P("section", "seq", None)),
        check_vma=False,
    )
```
